256 devices in a mesh: hid: 16 (over y, x_lo, core), wid: 16 (over z, x_hi).
Axes of the slice: x: 4 (x_hi: 2, x_lo: 2; x = x_hi * 2 + x_lo), y: 4, z: 8, core: 2. Of those that a mesh axis runs over, the one named last changes fastest.
Arguments:
- tokens: bfloat16 [512, 8192], P('hid', 'wid'), may hold values from -6 to 6
- out_grad: bfloat16 [512, 8192], P('hid', 'wid'), may hold values from -6 to 6
- gate_weight: bfloat16 [8192, 28672], P('wid', 'hid'), may hold values from -0.0625 to 0.0625
- up_weight: bfloat16 [8192, 28672], P('wid', 'hid'), may hold values from -0.0625 to 0.0625
- down_weight: bfloat16 [28672, 8192], P('hid', 'wid'), may hold values from -0.03125 to 0.03125
- cap_codes: int32 [28672], P('hid'), may hold values from 256 to 2048
Outputs:
- input_grad: bfloat16 [512, 8192], P('hid', 'wid')
- gate_grad: bfloat16 [8192, 28672], P('wid', 'hid')
- up_grad: bfloat16 [8192, 28672], P('wid', 'hid')
- down_grad: bfloat16 [28672, 8192], P('hid', 'wid')
The draws below stay inside these ranges and needn't reach their ends.
Inputs may be any that keep to these rules, and one draw needn't show every extreme that they name: `cap_codes`: each hidden unit's cap is its code divided by 512.
All inputs are finite; a program needn't handle non-finite values.
Results may differ from the reference program's by a relative error of at most 0.005.
Values may be sent and summed in bfloat16 or wider, within the bound.
A program may use at most 128 MiB of HBM per device.

```python
import jax
import jax.numpy as jnp

D = 8192
FF = 28672
TOKENS = 512


def place_ends(values, rng, least, largest):
    index_at = [jax.random.randint(jax.random.fold_in(rng, axis), (), 0, length) for axis, length in enumerate(values.shape)]
    main_axis = values.shape.index(max(values.shape))
    neighbour = index_at[:main_axis] + [(index_at[main_axis] + 1) % values.shape[main_axis]] + index_at[main_axis + 1:]
    return values.at[tuple(index_at)].set(least).at[tuple(neighbour)].set(largest)


def steps_of(key, extent, pieces, low, high):
    def one(axis_at, blocks):
        steps = jax.random.uniform(jax.random.fold_in(jax.random.fold_in(key, 6), axis_at), (blocks,), jnp.float32, low / len(pieces), high / len(pieces))
        return jnp.repeat(jnp.exp(steps), extent[axis_at] // blocks).reshape((-1,) + (1,) * (len(extent) - axis_at - 1))

    level = one(*pieces[0])
    for cut in pieces[1:]:
        level = level * one(*cut)
    return level


def bell_draw(stream_key, dims, deviation, limit, cuts=(), dtype=jnp.bfloat16):
    drawn = deviation * jax.random.normal(stream_key, dims, jnp.float32)
    if cuts:
        drawn = drawn * steps_of(stream_key, dims, cuts, -0.22, 0.18)
    return jnp.clip(drawn, -limit, limit).astype(dtype)


def setup_inputs(seed: int = 0) -> dict:
    seeds = jax.random.split(jax.random.key(seed), 7)
    tokens = bell_draw(seeds[0], (TOKENS, D), 1.0, 6.0, ((0, 16), (1, 16)))
    out_grad = bell_draw(seeds[1], (TOKENS, D), 1.0, 6.0, ((0, 16), (1, 16)))
    gate_weight = bell_draw(seeds[2], (D, FF), D ** -0.5, 0.0625, ((0, 16), (1, 16)))
    up_weight = bell_draw(seeds[3], (D, FF), D ** -0.5, 0.0625, ((0, 16), (1, 16)))
    down_weight = bell_draw(seeds[4], (FF, D), FF ** -0.5, 0.03125, ((0, 16), (1, 16)))
    cap_codes = place_ends(jax.random.randint(seeds[5], (FF,), 256, 2049), jax.random.fold_in(seeds[5], 1), 256, 2048).astype(jnp.int32)
    return dict(tokens=tokens, out_grad=out_grad, gate_weight=gate_weight, up_weight=up_weight, down_weight=down_weight, cap_codes=cap_codes)


def reference(tokens, out_grad, gate_weight, up_weight, down_weight, cap_codes):
    gate = jnp.dot(tokens, gate_weight, preferred_element_type=jnp.float32)
    up = jnp.dot(tokens, up_weight, preferred_element_type=jnp.float32)
    cap_vals = cap_codes.astype(jnp.float32) * (1.0 / 512.0)
    sigmoid_gate = jax.nn.sigmoid(gate)
    active = gate * sigmoid_gate
    squash = jnp.tanh(active * up / cap_vals[None, :])
    capped = (cap_vals[None, :] * squash).astype(jnp.bfloat16)
    cap_grad = jnp.dot(out_grad, down_weight.T, preferred_element_type=jnp.float32)
    hidden_grad = cap_grad * (1.0 - squash * squash)
    gate_delta = (hidden_grad * up * sigmoid_gate * (1.0 + gate * (1.0 - sigmoid_gate))).astype(jnp.bfloat16)
    up_delta = (hidden_grad * active).astype(jnp.bfloat16)
    input_grad = (jnp.dot(gate_delta, gate_weight.T, preferred_element_type=jnp.float32)
                  + jnp.dot(up_delta, up_weight.T, preferred_element_type=jnp.float32)).astype(jnp.bfloat16)
    gate_grad = jnp.dot(tokens.T, gate_delta, preferred_element_type=jnp.float32).astype(jnp.bfloat16)
    up_grad = jnp.dot(tokens.T, up_delta, preferred_element_type=jnp.float32).astype(jnp.bfloat16)
    down_grad = jnp.dot(capped.T, out_grad, preferred_element_type=jnp.float32).astype(jnp.bfloat16)
    return (input_grad, gate_grad, up_grad, down_grad)
```

```python
import functools

import jax
import jax.numpy as jnp
from jax import lax
from jax.experimental import pallas as pl
from jax.experimental.pallas import tpu as pltpu
from jax.sharding import PartitionSpec as P

MESH = pl.DeviceIdType.MESH
BF16 = jnp.bfloat16
F32 = jnp.float32

TILE = 256
NB = 32
NZ = 8
SCALE = 2.0**18


def dot(a, b, ca, cb):
    return lax.dot_general(a, b, (((ca,), (cb,)), ((), ())), preferred_element_type=F32)


def enc(v):
    u = v * SCALE
    return ((u * jnp.abs(u)) * (u * u)).astype(BF16)


def dec(y):
    y = y.astype(F32)
    root = lax.rsqrt(lax.rsqrt(jnp.maximum(jnp.abs(y), 2e-38)))
    return root * jnp.where(y < 0.0, -1.0 / SCALE, 1.0 / SCALE)


def kernel(
    na, nb,
    tok_in, og_in, gw_in, uw_in, dw_in, cap_in,
    d_out, panel_out, ig_out,
    gw, uw, dw, panel,
    pa, pb, xa_s, xa_r, sa, ra, sb, rb, xb_s, xb_r,
    ga, gb, ig_acc, sib_s, sib_r, ig_s, ig_r,
    lsem, dsem, tok_ss, tok_rs, fwd_ss, fwd_rs, xa_ss, xa_rs, za_ss, za_rs, zb_ss, zb_rs, xb_ss, xb_rs,
    gxa_ss, gxa_rs, gza_ss, gza_rs, gzb_ss, gzb_rs, gxb_ss, gxb_rs, sib_ss, sib_rs, ig_ss, ig_rs,
):
    wa, wb = na * TILE, nb * TILE
    h, w = lax.axis_index("hid"), lax.axis_index("wid")
    z, xh = w // 2, w % 2
    xo = 1 - xh
    q, core = h // 2, h % 2
    zp = lambda k: (z + k + NZ) % NZ
    up_dev, dn_dev, x_dev = (h, zp(1) * 2 + xh), (h, zp(-1) * 2 + xh), (h, z * 2 + xo)
    z_dev = (dn_dev, up_dev)
    sib_dev = (q * 2 + 1 - core, w)
    chip = lambda j: (q + j + 8) % 8
    peer = lambda j: (chip(j) * 2 + core, w)

    def remote(src, dst, ss, rs, dev):
        return pltpu.make_async_remote_copy(
            src_ref=src, dst_ref=dst, send_sem=ss, recv_sem=rs, device_id=dev, device_id_type=MESH
        )

    loads = [
        pltpu.make_async_copy(tok_in, panel.at[0, q, core], lsem.at[0]),
        pltpu.make_async_copy(og_in, panel.at[1, q, core], lsem.at[1]),
        pltpu.make_async_copy(gw_in, gw, lsem.at[2]),
        pltpu.make_async_copy(uw_in, uw, lsem.at[3]),
        pltpu.make_async_copy(dw_in, dw, lsem.at[4]),
    ]
    for c in loads:
        c.start()

    bar = pltpu.get_barrier_semaphore()
    for dev in (up_dev, dn_dev, x_dev, sib_dev):
        pl.semaphore_signal(bar, inc=1, device_id=dev, device_id_type=MESH)
    for j in range(1, 8):
        pl.semaphore_signal(bar, inc=1, device_id=peer(j), device_id_type=MESH)
    pl.semaphore_wait(bar, 11)

    def tok_copy(p, j):
        mine = panel.at[p, q, core]
        return remote(mine, mine, tok_ss.at[p, j], tok_rs.at[p, j], peer(j))

    def fwd_copy(p, j):
        blk = panel.at[p, chip(-j), core]
        return remote(blk, blk, fwd_ss.at[p, j], fwd_rs.at[p, j], sib_dev)

    def fwd_got(p, j):
        blk = panel.at[p, chip(-j), 1 - core]
        return remote(blk, blk, fwd_ss.at[p, j], fwd_rs.at[p, j], sib_dev)

    for p in range(2):
        loads[p].wait()

        @pl.loop(1, 8)
        def _(j, p=p):
            tok_copy(p, j).start()

        fwd_copy(p, 0).start()

    def gather(p):
        @pl.loop(1, 8)
        def _(j):
            tok_copy(p, j).wait_recv()
            fwd_copy(p, j).start()

        @pl.loop(0, 8)
        def _(j):
            fwd_got(p, j).wait_recv()

    def partial(m, rows, col):
        if m == 2:
            return dot(rows, dw[pl.ds(col, TILE), :], 1, 1)
        return dot(rows, (gw, uw)[m][:, pl.ds(col, TILE)], 1, 0)

    def tile(i):
        return pl.ds(pl.multiple_of(i * TILE, TILE), TILE)

    def part_a(ms, dst, x, f):
        @pl.loop(0, na)
        def _(i):
            for m in ms:
                rows = panel[m // 2, :, x].reshape(NZ * NB, 512)
                dst[:, m, :, tile(i)] = f(partial(m, rows, pl.multiple_of(i * TILE, TILE))).reshape(NZ, NB, TILE)

    def part_b(ms):
        @pl.loop(0, nb)
        def _(i):
            for m in ms:
                rows = panel[m // 2].reshape(2 * NZ * NB, 512)
                v = partial(m, rows, pl.multiple_of(wa + i * TILE, TILE)).reshape(NZ, 2, NB, TILE)
                for x in range(2):
                    pb[:, 3 * x + m, :, tile(i)] = v[:, x]

    def xa_copy(k, g):
        d = zp(k)
        ms = (pl.ds(0, 2), pl.ds(2, 1))[g]
        return remote(xa_s.at[d, ms], xa_r.at[d, ms], xa_ss.at[g, d], xa_rs.at[g, d], x_dev)

    order = (4, 3, -3, 2, -2, 1, -1, 0)
    gather(0)
    loads[2].wait()
    loads[3].wait()
    part_a((0, 1), xa_s, xo, enc)
    for k in order[:2]:
        xa_copy(k, 0).start()
    part_b((0, 1))
    part_a((0, 1), pa, xh, lambda v: v)
    gather(1)
    loads[4].wait()
    part_a((2,), xa_s, xo, enc)
    for k in order[:2]:
        xa_copy(k, 1).start()
    for k in order[2:]:
        for g in range(2):
            xa_copy(k, g).start()
    part_b((2,))

    def hop(dst, own, recv, lo, hi):
        width = own.shape[-1] // 2

        @pl.loop(0, own.shape[0])
        def _(m):
            @pl.loop(lo, hi)
            def _(i):
                c = pl.ds(pl.multiple_of(i * width, 128), width)
                v = own[m, :, c]
                for r in recv:
                    v = v + dec(r[m, :, c])
                dst[m, :, c] = enc(v) if dst.dtype == BF16 else v

    class Ring:
        def __init__(self, own, s, r, ss, rs):
            self.own, self.s, self.r, self.ss, self.rs = own, s, r, ss, rs
            self.half = own.shape[-1] // 2

        def copy(self, step, d):
            src, dst = self.s.at[d, step - 1], self.r.at[d, step - 1]
            if step == 1:
                c = pl.ds(d * self.half, self.half)
                src, dst = src.at[:, :, c], dst.at[:, :, c]
            return remote(src, dst, self.ss.at[d, step - 1], self.rs.at[d, step - 1], z_dev[d])

        def step(self, step):
            for d in range(2):
                own = self.own.at[zp((5 - step) * (-1, 1)[d])]
                src = self.s.at[d, step - 1]
                if step == 1:
                    hop(src, own, (), d, d + 1)
                else:
                    self.copy(step - 1, d).wait_recv()
                    got = self.r.at[d, step - 2]
                    if step == 2:
                        hop(src, own, (got,), d, d + 1)
                        hop(src, own, (), 1 - d, 2 - d)
                    else:
                        hop(src, own, (got,), 0, 2)
                self.copy(step, d).start()

        def finish(self, dst):
            for d in range(2):
                self.copy(4, d).wait_recv()
            hop(dst, self.own.at[z], (self.r.at[0, 3], self.r.at[1, 3]), 0, 2)

        def drain(self):
            for d in range(2):
                for step in range(1, 5):
                    self.copy(step, d).wait_send()

    ring_a = Ring(pa, sa, ra, za_ss, za_rs)
    ring_b = Ring(pb, sb, rb, zb_ss, zb_rs)

    ring_b.step(1)
    part_a((2,), pa, xh, lambda v: v)

    def take_x(k):
        for g in range(2):
            xa_copy(k, g).wait_recv()
        d = zp(k)
        hop(pa.at[d], pa.at[d], (xa_r.at[d],), 0, 2)

    take_x(4)
    ring_a.step(1)
    for s, ks in ((2, (3, -3)), (3, (2, -2)), (4, (1, -1))):
        ring_b.step(s)
        for k in ks:
            take_x(k)
        ring_a.step(s)
    ring_b.finish(pb.at[z])
    hop(xb_s, pb.at[z, pl.ds(3 * xo, 3)], (), 0, 2)
    xb_copy = remote(xb_s, xb_r, xb_ss, xb_rs, x_dev)
    xb_copy.start()
    take_x(0)
    ring_a.finish(pa.at[z])

    def local(src, dst, n, base):
        @pl.loop(0, n)
        def _(i):
            gate, up, cap_grad = src[0, :, tile(i)], src[1, :, tile(i)], src[2, :, tile(i)]
            at = 2 * (base + i)
            codes = jnp.concatenate([cap_in[pl.ds(at, 1), :], cap_in[pl.ds(at + 1, 1), :]], axis=1)
            cap = codes.astype(F32) * (1.0 / 512.0)
            sig = 1.0 / (1.0 + jnp.exp(-gate))
            act = gate * sig
            squash = jnp.tanh(act * up / cap)
            hid_grad = cap_grad * (1.0 - squash * squash)
            dst[0, :, tile(i)] = (cap * squash).astype(BF16)
            dst[1, :, tile(i)] = (hid_grad * up * sig * (1.0 + gate * (1.0 - sig))).astype(BF16)
            dst[2, :, tile(i)] = (hid_grad * act).astype(BF16)

    local(pa.at[z], ga.at[z, xh], na, 0)

    def halves(blk, step, d, width):
        return blk.at[:, :, pl.ds(d * (width // 2), width // 2)] if step == 4 else blk

    def gza_copy(step, d, got=False):
        blk = halves(ga.at[zp((step if got else step - 1) * (1, -1)[d]), xh], step, d, wa)
        return remote(blk, blk, gza_ss.at[d, step - 1], gza_rs.at[d, step - 1], z_dev[d])

    def gxa_copy(k, got=False):
        blk = ga.at[zp(k), xo if got else xh]
        return remote(blk, blk, gxa_ss.at[zp(k)], gxa_rs.at[zp(k)], x_dev)

    def gzb_copy(step, d, got=False):
        blk = halves(gb.at[zp((step if got else step - 1) * (1, -1)[d])], step, d, wb)
        return remote(blk, blk, gzb_ss.at[d, step - 1], gzb_rs.at[d, step - 1], z_dev[d])

    def keep_a(k, x):
        d = zp(k)
        t = pl.multiple_of((d * 2 + x) * NB, NB)
        return pltpu.make_async_copy(ga.at[d, x], d_out.at[:, pl.ds(t, NB), pl.ds(0, wa)], dsem.at[0, d, x])

    def keep_b(k, x):
        d = zp(k)
        t = pl.multiple_of((d * 2 + x) * NB, NB)
        return pltpu.make_async_copy(
            gb.at[d, pl.ds(3 * x, 3)], d_out.at[:, pl.ds(t, NB), pl.ds(wa, wb)], dsem.at[1, d, x]
        )

    def keep_bs(k):
        for x in range(2):
            keep_b(k, x).start()

    for d in range(2):
        gza_copy(1, d).start()
    gxa_copy(0).start()
    keep_a(0, xh).start()
    keep_panel = pltpu.make_async_copy(panel, panel_out, lsem.at[0])
    keep_panel.start()

    xb_copy.wait()
    own_b = pb.at[z, pl.ds(3 * xh, 3)]
    hop(own_b, own_b, (xb_r,), 0, 2)
    local(own_b, gb.at[z, pl.ds(3 * xh, 3)], nb, na)

    def gxb_copy(x):
        blk = gb.at[z, pl.ds(3 * x, 3)]
        return remote(blk, blk, gxb_ss, gxb_rs, x_dev)

    gxb_copy(xh).start()

    @pl.loop(0, NZ * 2)
    def _(i):
        ig_acc[i // 2, i % 2] = jnp.zeros((NB, 512), F32)

    def ig_rows(ks):
        def rows(ref, m, i):
            return jnp.concatenate([ref(zp(k), x, m, i) for k in ks for x in range(2)], axis=0)

        def run(ref, n, base):
            @pl.loop(0, n)
            def _(i):
                c = tile(base + i)
                v = dot(rows(ref, 1, i), gw[:, c], 1, 1) + dot(rows(ref, 2, i), uw[:, c], 1, 1)
                for n_k, k in enumerate(ks):
                    ig_acc[zp(k)] += v[n_k * 2 * NB : (n_k + 1) * 2 * NB].reshape(2, NB, 512)

        run(lambda d, x, m, i: ga[d, x, m, :, tile(i)], na, 0)
        run(lambda d, x, m, i: gb[d, 3 * x + m, :, tile(i)], nb, na)
        for k in ks:
            d = zp(k)
            sib_s[d] = ig_acc[d, 1 - core].astype(BF16)
            sib_copy(d).start()

    def sib_copy(d):
        return remote(sib_s.at[d], sib_r.at[d], sib_ss.at[d], sib_rs.at[d], sib_dev)

    def take_gx(k):
        gxa_copy(k, True).wait_recv()
        keep_a(k, xo).start()

    for step in range(2, 5):
        for d in range(2):
            k = (step - 1) * (1, -1)[d]
            gza_copy(step - 1, d, True).wait_recv()
            gza_copy(step, d).start()
            gxa_copy(k).start()
            keep_a(k, xh).start()
        if step == 2:
            gxb_copy(xo).wait_recv()
            keep_bs(0)
        for d in range(2):
            if step > 2:
                gzb_copy(step - 2, d, True).wait_recv()
                keep_bs((step - 2) * (1, -1)[d])
            gzb_copy(step - 1, d).start()
    for d in range(2):
        gza_copy(4, d, True).wait_recv()
    gxa_copy(4).start()
    keep_a(4, xh).start()
    for d in range(2):
        gzb_copy(3, d, True).wait_recv()
        gzb_copy(4, d).start()
        keep_bs(3 * (1, -1)[d])

    early, late = (0, 1, -1, 2, -2), (3, -3, 4)
    for k in early:
        take_gx(k)
    ig_rows(early)

    @pl.loop(1, 8)
    def _(j):
        for p in range(2):
            tok_copy(p, j).wait_send()

    @pl.loop(0, 8)
    def _(j):
        for p in range(2):
            fwd_copy(p, j).wait_send()
            xa_copy(j, p).wait_send()

    ring_a.drain()
    ring_b.drain()

    for k in late:
        take_gx(k)
    for d in range(2):
        gzb_copy(4, d, True).wait_recv()
    keep_bs(4)
    ig_rows(late)

    def ig_copy(j):
        return remote(ig_s.at[chip(j)], ig_r.at[j], ig_ss.at[j], ig_rs.at[j], peer(j))

    @pl.loop(1, 9)
    def _(j):
        d = chip(j)
        sib_copy(d).wait_recv()
        v = ig_acc[d, core] + sib_r[d].astype(F32)
        ig_acc[d, core] = v
        ig_s[d] = v.astype(BF16)

        @pl.when(j < 8)
        def _():
            ig_copy(j).start()

    @pl.loop(0, 8)
    def _(j):
        gxa_copy(j).wait_send()
        sib_copy(j).wait_send()

    for d in range(2):
        for step in range(1, 5):
            gza_copy(step, d).wait_send()
            gzb_copy(step, d).wait_send()
    gxb_copy(xh).wait_send()

    @pl.loop(1, 8)
    def _(j):
        ig_copy(j).wait()
        ig_acc[q, core] += ig_r[j].astype(F32)

    last = pltpu.make_async_copy(ig_acc.at[q, core], ig_out, lsem.at[1])
    last.start()

    @pl.loop(0, 8)
    def _(k):
        for x in range(2):
            keep_a(k, x).wait()
            keep_b(k, x).wait()

    keep_panel.wait()
    last.wait()


def weight_grads(d_in, panel, ig_in, ig_out, gg_out, ug_out, dg_out):
    gg_out[...] = dot(panel[0], d_in[1], 0, 0).astype(BF16)
    ug_out[...] = dot(panel[0], d_in[2], 0, 0).astype(BF16)
    dg_out[...] = dot(d_in[0], panel[1], 0, 0).astype(BF16)

    @pl.when(pl.program_id(0) == 0)
    def _():
        ig_out[...] = ig_in[...].astype(BF16)


def per_device(tokens, out_grad, gate_weight, up_weight, down_weight, cap_codes):
    hidden = gate_weight.shape[1]
    n = hidden // TILE
    na = 4
    nb = n - na
    wa, wb = na * TILE, nb * TILE
    dma = pltpu.SemaphoreType.DMA
    sh = jax.ShapeDtypeStruct
    scratch = [
        pltpu.VMEM((512, hidden), BF16),
        pltpu.VMEM((512, hidden), BF16),
        pltpu.VMEM((hidden, 512), BF16),
        pltpu.VMEM((2, NZ, 2, NB, 512), BF16),
        pltpu.VMEM((NZ, 3, NB, wa), F32),
        pltpu.VMEM((NZ, 6, NB, wb), F32),
        pltpu.VMEM((NZ, 3, NB, wa), BF16),
        pltpu.VMEM((NZ, 3, NB, wa), BF16),
        pltpu.VMEM((2, 4, 3, NB, wa), BF16),
        pltpu.VMEM((2, 4, 3, NB, wa), BF16),
        pltpu.VMEM((2, 4, 6, NB, wb), BF16),
        pltpu.VMEM((2, 4, 6, NB, wb), BF16),
        pltpu.VMEM((3, NB, wb), BF16),
        pltpu.VMEM((3, NB, wb), BF16),
        pltpu.VMEM((NZ, 2, 3, NB, wa), BF16),
        pltpu.VMEM((NZ, 6, NB, wb), BF16),
        pltpu.VMEM((NZ, 2, NB, 512), F32),
        pltpu.VMEM((NZ, NB, 512), BF16),
        pltpu.VMEM((NZ, NB, 512), BF16),
        pltpu.VMEM((NZ, NB, 512), BF16),
        pltpu.VMEM((NZ, NB, 512), BF16),
        dma((5,)), dma((2, NZ, 2)),
        dma((2, 8)), dma((2, 8)),
        dma((2, 8)), dma((2, 8)),
        dma((2, NZ)), dma((2, NZ)),
        dma((2, 4)), dma((2, 4)),
        dma((2, 4)), dma((2, 4)),
        dma, dma,
        dma((NZ,)), dma((NZ,)),
        dma((2, 4)), dma((2, 4)),
        dma((2, 4)), dma((2, 4)),
        dma, dma,
        dma((NZ,)), dma((NZ,)),
        dma((NZ,)), dma((NZ,)),
    ]
    any_spec = pl.BlockSpec(memory_space=pl.ANY)
    deltas, panel, ig_sum = pl.pallas_call(
        functools.partial(kernel, na, nb),
        out_shape=(sh((3, 512, hidden), BF16), sh((2, NZ, 2, NB, 512), BF16), sh((NB, 512), F32)),
        in_specs=[any_spec] * 5 + [pl.BlockSpec(memory_space=pltpu.VMEM)],
        out_specs=[any_spec] * 3,
        scratch_shapes=scratch,
        compiler_params=pltpu.CompilerParams(
            collective_id=0, has_side_effects=True, vmem_limit_bytes=60 << 20
        ),
        name="exchange",
    )(tokens, out_grad, gate_weight, up_weight, down_weight, cap_codes.reshape(hidden // 128, 128))
    wide = pl.BlockSpec((512, TILE), lambda i: (0, i))
    input_grad, gate_grad, up_grad, down_grad = pl.pallas_call(
        weight_grads,
        grid=(n,),
        out_shape=(
            sh((NB, 512), BF16),
            sh((512, hidden), BF16),
            sh((512, hidden), BF16),
            sh((hidden, 512), BF16),
        ),
        in_specs=[
            pl.BlockSpec((3, 512, TILE), lambda i: (0, 0, i)),
            pl.BlockSpec((2, 512, 512), lambda i: (0, 0, 0)),
            pl.BlockSpec((NB, 512), lambda i: (0, 0)),
        ],
        out_specs=(
            pl.BlockSpec((NB, 512), lambda i: (0, 0)),
            wide,
            wide,
            pl.BlockSpec((TILE, 512), lambda i: (i, 0)),
        ),
        compiler_params=pltpu.CompilerParams(vmem_limit_bytes=60 << 20),
        name="weight_grads",
    )(deltas, panel.reshape(2, 512, 512), ig_sum)
    return (input_grad, gate_grad, up_grad, down_grad)


def solution(mesh):
    return jax.shard_map(
        per_device,
        mesh=mesh,
        in_specs=(
            P("hid", "wid"),
            P("hid", "wid"),
            P("wid", "hid"),
            P("wid", "hid"),
            P("hid", "wid"),
            P("hid"),
        ),
        out_specs=(P("hid", "wid"), P("wid", "hid"), P("wid", "hid"), P("hid", "wid")),
        check_vma=False,
    )
```

```python
import functools

import jax
import jax.numpy as jnp
from jax import lax
from jax.experimental import pallas as pl
from jax.experimental.pallas import tpu as pltpu
from jax.sharding import PartitionSpec as P

MESH = pl.DeviceIdType.MESH
BF16 = jnp.bfloat16
F32 = jnp.float32

TILE = 256
NB = 32
NZ = 8
SCALE = 2.0**18


def dot(a, b, ca, cb):
    return lax.dot_general(a, b, (((ca,), (cb,)), ((), ())), preferred_element_type=F32)


def enc(v):
    u = v * SCALE
    return ((u * jnp.abs(u)) * (u * u)).astype(BF16)


def dec(y):
    y = y.astype(F32)
    root = lax.rsqrt(lax.rsqrt(jnp.maximum(jnp.abs(y), 2e-38)))
    return root * jnp.where(y < 0.0, -1.0 / SCALE, 1.0 / SCALE)


def kernel(
    na, nb,
    tok_in, og_in, gw_in, uw_in, dw_in, cap_in,
    d_out, panel_out, ig_out,
    gw, uw, dw, panel,
    pa, pb, xa_s, xa_r, sa, ra, sb, rb, xb_s, xb_r,
    ga, gb, ig_acc, sib_s, sib_r, ig_s, ig_r,
    lsem, dsem, tok_ss, tok_rs, fwd_ss, fwd_rs, xa_ss, xa_rs, za_ss, za_rs, zb_ss, zb_rs, xb_ss, xb_rs,
    gxa_ss, gxa_rs, gza_ss, gza_rs, gzb_ss, gzb_rs, gzb1_rs, gxb_ss, gxb_rs, sib_ss, sib_rs, ig_ss, ig_rs,
):
    wa, wb = na * TILE, nb * TILE
    h, w = lax.axis_index("hid"), lax.axis_index("wid")
    z, xh = w // 2, w % 2
    xo = 1 - xh
    q, core = h // 2, h % 2
    zp = lambda k: (z + k + NZ) % NZ
    up_dev, dn_dev, x_dev = (h, zp(1) * 2 + xh), (h, zp(-1) * 2 + xh), (h, z * 2 + xo)
    z_dev = (dn_dev, up_dev)
    sib_dev = (q * 2 + 1 - core, w)
    chip = lambda j: (q + j + 8) % 8
    peer = lambda j: (chip(j) * 2 + core, w)

    def remote(src, dst, ss, rs, dev):
        return pltpu.make_async_remote_copy(
            src_ref=src, dst_ref=dst, send_sem=ss, recv_sem=rs, device_id=dev, device_id_type=MESH
        )

    loads = [
        pltpu.make_async_copy(tok_in, panel.at[0, q, core], lsem.at[0]),
        pltpu.make_async_copy(og_in, panel.at[1, q, core], lsem.at[1]),
        pltpu.make_async_copy(gw_in, gw, lsem.at[2]),
        pltpu.make_async_copy(uw_in, uw, lsem.at[3]),
        pltpu.make_async_copy(dw_in, dw, lsem.at[4]),
    ]
    for c in loads:
        c.start()

    bar = pltpu.get_barrier_semaphore()
    for dev in (up_dev, dn_dev, x_dev, sib_dev):
        pl.semaphore_signal(bar, inc=1, device_id=dev, device_id_type=MESH)
    for j in range(1, 8):
        pl.semaphore_signal(bar, inc=1, device_id=peer(j), device_id_type=MESH)
    pl.semaphore_wait(bar, 11)

    def tok_copy(p, j):
        mine = panel.at[p, q, core]
        return remote(mine, mine, tok_ss, tok_rs.at[p, j], peer(j))

    def fwd_copy(p, j):
        blk = panel.at[p, chip(-j), core]
        return remote(blk, blk, fwd_ss, fwd_rs.at[p, j], sib_dev)

    def fwd_got(p, j):
        blk = panel.at[p, chip(-j), 1 - core]
        return remote(blk, blk, fwd_ss, fwd_rs.at[p, j], sib_dev)

    def send(p):
        loads[p].wait()

        @pl.loop(1, 8)
        def _(j):
            tok_copy(p, j).start()

        fwd_copy(p, 0).start()

    def forward(p):
        @pl.loop(1, 8)
        def _(j):
            tok_copy(p, j).wait_recv()
            fwd_copy(p, j).start()

    def gathered(p):
        @pl.loop(0, 8)
        def _(j):
            fwd_got(p, j).wait_recv()

    def partial(m, rows, col):
        if m == 2:
            return dot(rows, dw[pl.ds(col, TILE), :], 1, 1)
        return dot(rows, (gw, uw)[m][:, pl.ds(col, TILE)], 1, 0)

    def tile(i):
        return pl.ds(i * TILE, TILE)

    def part_a(ms, dst, x, f):
        for m in ms:
            rows = panel[m // 2, :, x].reshape(NZ * NB, 512)
            for i in range(na):
                dst[:, m, :, tile(i)] = f(partial(m, rows, i * TILE)).reshape(NZ, NB, TILE)

    def part_b(ms):
        for m in ms:
            rows = panel[m // 2].reshape(2 * NZ * NB, 512)
            for i in range(nb):
                v = partial(m, rows, wa + i * TILE).reshape(NZ, 2, NB, TILE)
                for x in range(2):
                    pb[:, 3 * x + m, :, tile(i)] = v[:, x]

    def xa_copy(k, g):
        d = zp(k)
        ms = (pl.ds(0, 2), pl.ds(2, 1))[g]
        return remote(xa_s.at[d, ms], xa_r.at[d, ms], xa_ss, xa_rs.at[g, d], x_dev)

    order = (4, 3, -3, 2, -2, 1, -1, 0)
    send(0)
    send(1)
    forward(0)
    forward(1)
    gathered(0)
    loads[2].wait()
    loads[3].wait()
    part_a((0, 1), xa_s, xo, enc)
    for k in order[:2]:
        xa_copy(k, 0).start()
    part_b((0, 1))
    gathered(1)
    loads[4].wait()
    part_a((2,), xa_s, xo, enc)
    for k in order[:2]:
        xa_copy(k, 1).start()
    for k in order[2:]:
        for g in range(2):
            xa_copy(k, g).start()
    part_b((2,))

    def hop(dst, own, recv, lo, hi):
        width = own.shape[-1] // 2

        @pl.loop(0, own.shape[0])
        def _(m):
            for i in range(lo, hi):
                c = pl.ds(i * width, width)
                v = own[m, :, c]
                for r in recv:
                    v = v + dec(r[m, :, c])
                dst[m, :, c] = enc(v) if dst.dtype == BF16 else v

    class Ring:
        def __init__(self, own, s, r, ss, rs):
            self.own, self.s, self.r, self.ss, self.rs = own, s, r, ss, rs
            self.half = own.shape[-1] // 2

        def copy(self, step, d):
            src, dst = self.s.at[d, step - 1], self.r.at[d, step - 1]
            if step == 1:
                c = pl.ds(d * self.half, self.half)
                src, dst = src.at[:, :, c], dst.at[:, :, c]
            return remote(src, dst, self.ss.at[min(step - 1, 1)], self.rs.at[d, step - 1], z_dev[d])

        def step(self, step):
            for d in range(2):
                own = self.own.at[zp((5 - step) * (-1, 1)[d])]
                src = self.s.at[d, step - 1]
                if step == 1:
                    hop(src, own, (), d, d + 1)
                else:
                    self.copy(step - 1, d).wait_recv()
                    got = self.r.at[d, step - 2]
                    if step == 2:
                        hop(src, own, (got,), d, d + 1)
                        hop(src, own, (), 1 - d, 2 - d)
                    else:
                        hop(src, own, (got,), 0, 2)
                self.copy(step, d).start()

        def finish(self, dst):
            for d in range(2):
                self.copy(4, d).wait_recv()
            hop(dst, self.own.at[z], (self.r.at[0, 3], self.r.at[1, 3]), 0, 2)

        def drain(self):
            one, rest = self.s.at[0, 0], self.s.at[:, pl.ds(1, 3)]
            remote(one, one, self.ss.at[0], self.rs.at[0, 0], z_dev[0]).wait_send()
            remote(rest, rest, self.ss.at[1], self.rs.at[0, 0], z_dev[0]).wait_send()

    ring_a = Ring(pa, sa, ra, za_ss, za_rs)
    ring_b = Ring(pb, sb, rb, zb_ss, zb_rs)

    ring_b.step(1)
    part_a((0, 1, 2), pa, xh, lambda v: v)

    def take_x(k):
        for g in range(2):
            xa_copy(k, g).wait_recv()
        d = zp(k)
        hop(pa.at[d], pa.at[d], (xa_r.at[d],), 0, 2)

    ring_b.step(2)
    take_x(4)
    ring_a.step(1)
    for s, ks in ((2, (3, -3)), (3, (2, -2))):
        ring_b.step(s + 1)
        for k in ks:
            take_x(k)
        ring_a.step(s)
    ring_b.finish(pb.at[z])
    hop(xb_s, pb.at[z, pl.ds(3 * xo, 3)], (), 0, 2)
    xb_copy = remote(xb_s, xb_r, xb_ss, xb_rs, x_dev)
    xb_copy.start()
    for k in (1, -1):
        take_x(k)
    ring_a.step(4)
    take_x(0)

    def local(src, dst, n, base):
        for i in range(n):
            gate, up, cap_grad = src[0, :, tile(i)], src[1, :, tile(i)], src[2, :, tile(i)]
            at = 2 * (base + i)
            codes = jnp.concatenate([cap_in[at : at + 1, :], cap_in[at + 1 : at + 2, :]], axis=1)
            cap = codes.astype(F32) * (1.0 / 512.0)
            sig = 1.0 / (1.0 + jnp.exp(-gate))
            act = gate * sig
            squash = jnp.tanh(act * up / cap)
            hid_grad = cap_grad * (1.0 - squash * squash)
            dst[0, :, tile(i)] = (cap * squash).astype(BF16)
            dst[1, :, tile(i)] = (hid_grad * up * sig * (1.0 + gate * (1.0 - sig))).astype(BF16)
            dst[2, :, tile(i)] = (hid_grad * act).astype(BF16)

    xb_copy.wait()
    own_b = pb.at[z, pl.ds(3 * xh, 3)]
    hop(own_b, own_b, (xb_r,), 0, 2)
    local(own_b, gb.at[z, pl.ds(3 * xh, 3)], nb, na)

    def gxb_copy(x):
        blk = gb.at[z, pl.ds(3 * x, 3)]
        return remote(blk, blk, gxb_ss, gxb_rs, x_dev)

    gxb_copy(xh).start()
    ring_a.finish(pa.at[z])
    local(pa.at[z], ga.at[z, xh], na, 0)

    def halves(blk, step, d, width):
        return blk.at[:, :, pl.ds(d * (width // 2), width // 2)] if step == 4 else blk

    def gza_copy(step, d, got=False):
        blk = halves(ga.at[zp((step if got else step - 1) * (1, -1)[d]), xh], step, d, wa)
        return remote(blk, blk, gza_ss.at[step // 4], gza_rs.at[d, step - 1], z_dev[d])

    def gxa_copy(k, got=False):
        blk = ga.at[zp(k), xo if got else xh]
        return remote(blk, blk, gxa_ss, gxa_rs.at[zp(k)], x_dev)

    def gzb_copy(step, d, got=False):
        blk = halves(gb.at[zp((step if got else step - 1) * (1, -1)[d])], step, d, wb)
        return remote(blk, blk, gzb_ss.at[step // 4], gzb_rs.at[d, step - 1], z_dev[d])

    def gzb_first(d, x, got=False):
        blk = gb.at[zp((1, -1)[d] if got else 0), pl.ds(3 * x, 3)]
        return remote(blk, blk, gzb_ss.at[0], gzb1_rs.at[d, x], z_dev[d])

    def keep_a(k, x):
        d = zp(k)
        t = pl.multiple_of((d * 2 + x) * NB, NB)
        return pltpu.make_async_copy(ga.at[d, x], d_out.at[:, pl.ds(t, NB), pl.ds(0, wa)], dsem.at[0])

    def keep_b(k, x):
        d = zp(k)
        t = pl.multiple_of((d * 2 + x) * NB, NB)
        return pltpu.make_async_copy(
            gb.at[d, pl.ds(3 * x, 3)], d_out.at[:, pl.ds(t, NB), pl.ds(wa, wb)], dsem.at[1]
        )

    def keep_bs(k):
        for x in range(2):
            keep_b(k, x).start()

    for d in range(2):
        gza_copy(1, d).start()
    gxa_copy(0).start()
    for d in range(2):
        gzb_first(d, xh).start()
    keep_a(0, xh).start()
    keep_panel = pltpu.make_async_copy(panel, panel_out, lsem.at[0])
    keep_panel.start()

    def ig_rows(ks):
        def rows(ref):
            return jnp.concatenate([ref(zp(k), x) for k in ks for x in range(2)], axis=0)

        v = 0.0
        for m, wt in ((1, gw), (2, uw)):
            v = v + dot(rows(lambda d, x: ga[d, x, m]), wt[:, :wa], 1, 1)
            v = v + dot(rows(lambda d, x: gb[d, 3 * x + m]), wt[:, wa:], 1, 1)
        for n_k, k in enumerate(ks):
            ig_acc[zp(k)] = v[n_k * 2 * NB : (n_k + 1) * 2 * NB].reshape(2, NB, 512)
        for k in ks:
            d = zp(k)
            sib_s[d] = ig_acc[d, 1 - core].astype(BF16)
            sib_copy(d).start()

    def ig_send(ks):
        for k in ks:
            d = zp(k)
            sib_copy(d).wait_recv()
            v = ig_acc[d, core] + sib_r[d].astype(F32)
            ig_acc[d, core] = v
            ig_s[d] = v.astype(BF16)

            @pl.when(d != q)
            def _():
                ig_copy((d - q + 8) % 8).start()

    def ig_copy(j):
        return remote(ig_s.at[chip(j)], ig_r.at[j], ig_ss, ig_rs.at[j], peer(j))

    def sib_copy(d):
        return remote(sib_s.at[d], sib_r.at[d], sib_ss, sib_rs.at[d], sib_dev)

    def take_gx(k):
        gxa_copy(k, True).wait_recv()
        keep_a(k, xo).start()

    def forward_a(step):
        for d in range(2):
            k = (step - 1) * (1, -1)[d]
            gza_copy(step - 1, d, True).wait_recv()
            gza_copy(step, d).start()
            gxa_copy(k).start()
            keep_a(k, xh).start()

    def forward_b(step):
        for d in range(2):
            if step == 2:
                for x in range(2):
                    gzb_first(d, x, True).wait_recv()
            else:
                gzb_copy(step - 1, d, True).wait_recv()
            gzb_copy(step, d).start()
            keep_bs((step - 1) * (1, -1)[d])

    forward_a(2)
    gxb_copy(xo).wait_recv()
    for d in range(2):
        gzb_first(d, xo).start()
    keep_bs(0)
    forward_a(3)
    forward_b(2)
    forward_a(4)
    forward_b(3)

    def sent(ref, sem):
        remote(ref, ref, sem, gxb_rs, x_dev).wait_send()

    sent(panel.at[0, pl.ds(0, 7)], tok_ss)
    sent(panel.at[0], fwd_ss)
    sent(xa_s, xa_ss)
    ring_a.drain()
    ring_b.drain()
    early = (0, 1, -1, 2, -2)
    for k in early:
        take_gx(k)
    ig_rows(early)
    for d in range(2):
        gza_copy(4, d, True).wait_recv()
    gxa_copy(4).start()
    keep_a(4, xh).start()
    ig_send(early)
    forward_b(4)
    for k in (3, -3):
        take_gx(k)
    ig_rows((3, -3))
    ig_send((3, -3))
    take_gx(4)
    for d in range(2):
        gzb_copy(4, d, True).wait_recv()
    keep_bs(4)
    ig_rows((4,))
    ig_send((4,))

    sent(xa_s, gxa_ss)
    sent(sib_s, sib_ss)
    sent(sa.at[0, 0], gza_ss.at[1])
    sent(sa.at[:, pl.ds(0, 3)], gza_ss.at[0])
    sent(sb.at[0, 0], gzb_ss.at[1])
    sent(sb.at[:, pl.ds(0, 3)], gzb_ss.at[0])
    gxb_copy(xh).wait_send()

    @pl.loop(1, 8)
    def _(j):
        ig_copy(j).wait_recv()
        ig_acc[q, core] += ig_r[j].astype(F32)

    sent(ig_s.at[pl.ds(0, 7)], ig_ss)
    last = pltpu.make_async_copy(ig_acc.at[q, core], ig_out, lsem.at[1])
    last.start()

    pltpu.make_async_copy(ga, ga, dsem.at[0]).wait()
    pltpu.make_async_copy(gb, gb, dsem.at[1]).wait()
    keep_panel.wait()
    last.wait()


def weight_grads(d_in, panel_in, ig_in, ig_out, gg_out, ug_out, dg_out, d, panel, gg, ug, dg, isem, osem):
    loads = {}
    for at, (src, dst) in enumerate(
        (
            (panel_in.at[0], panel.at[0]),
            (d_in.at[1], d.at[1]),
            (d_in.at[2], d.at[2]),
            (panel_in.at[1], panel.at[1]),
            (d_in.at[0], d.at[0]),
        )
    ):
        loads[at] = pltpu.make_async_copy(src, dst, isem.at[at])
        loads[at].start()
    ig_out[...] = ig_in[...].astype(BF16)
    n = d.shape[2] // TILE
    stores = []

    def store(src, dst):
        stores.append(pltpu.make_async_copy(src, dst, osem.at[len(stores)]))
        stores[-1].start()

    loads[0].wait()
    for m, dst, out in ((1, gg, gg_out), (2, ug, ug_out)):
        loads[m].wait()
        for i in range(n):
            c = pl.ds(i * TILE, TILE)
            dst[:, c] = dot(panel[0], d[m, :, c], 0, 0).astype(BF16)
        store(dst, out)
    loads[3].wait()
    loads[4].wait()
    for lo, hi in ((0, 4), (4, 6), (6, 7)):
        for i in range(lo, hi):
            c = pl.ds(i * TILE, TILE)
            dg[c, :] = dot(d[0, :, c], panel[1], 0, 0).astype(BF16)
        rows = pl.ds(lo * TILE, (hi - lo) * TILE)
        store(dg.at[rows], dg_out.at[rows])
    for c in stores:
        c.wait()


def per_device(tokens, out_grad, gate_weight, up_weight, down_weight, cap_codes):
    hidden = gate_weight.shape[1]
    n = hidden // TILE
    na = 4
    nb = n - na
    wa, wb = na * TILE, nb * TILE
    dma = pltpu.SemaphoreType.DMA
    sh = jax.ShapeDtypeStruct
    scratch = [
        pltpu.VMEM((512, hidden), BF16),
        pltpu.VMEM((512, hidden), BF16),
        pltpu.VMEM((hidden, 512), BF16),
        pltpu.VMEM((2, NZ, 2, NB, 512), BF16),
        pltpu.VMEM((NZ, 3, NB, wa), F32),
        pltpu.VMEM((NZ, 6, NB, wb), F32),
        pltpu.VMEM((NZ, 3, NB, wa), BF16),
        pltpu.VMEM((NZ, 3, NB, wa), BF16),
        pltpu.VMEM((2, 4, 3, NB, wa), BF16),
        pltpu.VMEM((2, 4, 3, NB, wa), BF16),
        pltpu.VMEM((2, 4, 6, NB, wb), BF16),
        pltpu.VMEM((2, 4, 6, NB, wb), BF16),
        pltpu.VMEM((3, NB, wb), BF16),
        pltpu.VMEM((3, NB, wb), BF16),
        pltpu.VMEM((NZ, 2, 3, NB, wa), BF16),
        pltpu.VMEM((NZ, 6, NB, wb), BF16),
        pltpu.VMEM((NZ, 2, NB, 512), F32),
        pltpu.VMEM((NZ, NB, 512), BF16),
        pltpu.VMEM((NZ, NB, 512), BF16),
        pltpu.VMEM((NZ, NB, 512), BF16),
        pltpu.VMEM((NZ, NB, 512), BF16),
        dma((5,)), dma((2,)),
        dma, dma((2, 8)),
        dma, dma((2, 8)),
        dma, dma((2, NZ)),
        dma((2,)), dma((2, 4)),
        dma((2,)), dma((2, 4)),
        dma, dma,
        dma, dma((NZ,)),
        dma((2,)), dma((2, 4)),
        dma((2,)), dma((2, 4)), dma((2, 2)),
        dma, dma,
        dma, dma((NZ,)),
        dma, dma((NZ,)),
    ]
    any_spec = pl.BlockSpec(memory_space=pl.ANY)
    deltas, panel, ig_sum = pl.pallas_call(
        functools.partial(kernel, na, nb),
        out_shape=(sh((3, 512, hidden), BF16), sh((2, NZ, 2, NB, 512), BF16), sh((NB, 512), F32)),
        in_specs=[any_spec] * 5 + [pl.BlockSpec(memory_space=pltpu.VMEM)],
        out_specs=[any_spec] * 3,
        scratch_shapes=scratch,
        compiler_params=pltpu.CompilerParams(
            collective_id=0, has_side_effects=True, vmem_limit_bytes=60 << 20
        ),
        name="exchange",
    )(tokens, out_grad, gate_weight, up_weight, down_weight, cap_codes.reshape(hidden // 128, 128))
    return pl.pallas_call(
        weight_grads,
        out_shape=(
            sh((NB, 512), BF16),
            sh((512, hidden), BF16),
            sh((512, hidden), BF16),
            sh((hidden, 512), BF16),
        ),
        in_specs=[any_spec, any_spec, pl.BlockSpec(memory_space=pltpu.VMEM)],
        out_specs=(pl.BlockSpec(memory_space=pltpu.VMEM), any_spec, any_spec, any_spec),
        scratch_shapes=[
            pltpu.VMEM((3, 512, hidden), BF16),
            pltpu.VMEM((2, 512, 512), BF16),
            pltpu.VMEM((512, hidden), BF16),
            pltpu.VMEM((512, hidden), BF16),
            pltpu.VMEM((hidden, 512), BF16),
            dma((5,)),
            dma((5,)),
        ],
        compiler_params=pltpu.CompilerParams(vmem_limit_bytes=60 << 20),
        name="weight_grads",
    )(deltas, panel.reshape(2, 512, 512), ig_sum)


def solution(mesh):
    return jax.shard_map(
        per_device,
        mesh=mesh,
        in_specs=(
            P("hid", "wid"),
            P("hid", "wid"),
            P("wid", "hid"),
            P("wid", "hid"),
            P("hid", "wid"),
            P("hid"),
        ),
        out_specs=(P("hid", "wid"), P("wid", "hid"), P("wid", "hid"), P("hid", "wid")),
        check_vma=False,
    )
```

```python
import functools

import jax
import jax.numpy as jnp
from jax import lax
from jax.experimental import pallas as pl
from jax.experimental.pallas import tpu as pltpu
from jax.sharding import PartitionSpec as P

MESH = pl.DeviceIdType.MESH
BF16 = jnp.bfloat16
F32 = jnp.float32

TILE = 256
NB = 32
NZ = 8
SCALE = 2.0**18


def dot(a, b, ca, cb):
    return lax.dot_general(a, b, (((ca,), (cb,)), ((), ())), preferred_element_type=F32)


def enc(v):
    u = v * SCALE
    return ((u * jnp.abs(u)) * (u * u)).astype(BF16)


def dec(y):
    y = y.astype(F32)
    root = lax.rsqrt(lax.rsqrt(jnp.maximum(jnp.abs(y), 2e-38)))
    return root * jnp.where(y < 0.0, -1.0 / SCALE, 1.0 / SCALE)


def kernel(
    na, nb,
    tok_in, og_in, gw_in, uw_in, dw_in, cap_in,
    d_out, panel_out, ig_out,
    gw, uw, dw, panel,
    pa, pb, xa_s, xa_r, sa, ra, sb, rb, xb_s, xb_r,
    ga, gb, ig_acc, sib_s, sib_r, ig_s, ig_r,
    lsem, dsem, tok_ss, tok_rs, fwd_ss, fwd_rs, xa_ss, xa_rs, za_ss, za_rs, zb_ss, zb_rs, xb_ss, xb_rs,
    gxa_ss, gxa_rs, gza_ss, gza_rs, gzb_ss, gzb_rs, gxb_ss, gxb_rs, sib_ss, sib_rs, ig_ss, ig_rs,
):
    wa, wb = na * TILE, nb * TILE
    h, w = lax.axis_index("hid"), lax.axis_index("wid")
    z, xh = w // 2, w % 2
    xo = 1 - xh
    q, core = h // 2, h % 2
    zp = lambda k: (z + k + NZ) % NZ
    up_dev, dn_dev, x_dev = (h, zp(1) * 2 + xh), (h, zp(-1) * 2 + xh), (h, z * 2 + xo)
    z_dev = (dn_dev, up_dev)
    sib_dev = (q * 2 + 1 - core, w)
    chip = lambda j: (q + j + 8) % 8
    peer = lambda j: (chip(j) * 2 + core, w)

    def remote(src, dst, ss, rs, dev):
        return pltpu.make_async_remote_copy(
            src_ref=src, dst_ref=dst, send_sem=ss, recv_sem=rs, device_id=dev, device_id_type=MESH
        )

    loads = [
        pltpu.make_async_copy(tok_in, panel.at[0, q, core], lsem.at[0]),
        pltpu.make_async_copy(og_in, panel.at[1, q, core], lsem.at[1]),
        pltpu.make_async_copy(gw_in, gw, lsem.at[2]),
        pltpu.make_async_copy(uw_in, uw, lsem.at[3]),
        pltpu.make_async_copy(dw_in, dw, lsem.at[4]),
    ]
    for c in loads:
        c.start()

    bar = pltpu.get_barrier_semaphore()
    for dev in (up_dev, dn_dev, x_dev, sib_dev):
        pl.semaphore_signal(bar, inc=1, device_id=dev, device_id_type=MESH)
    for j in range(1, 8):
        pl.semaphore_signal(bar, inc=1, device_id=peer(j), device_id_type=MESH)
    pl.semaphore_wait(bar, 11)

    def tok_copy(p, j):
        mine = panel.at[p, q, core]
        return remote(mine, mine, tok_ss, tok_rs.at[p, j], peer(j))

    def fwd_copy(p, j):
        blk = panel.at[p, chip(-j), core]
        return remote(blk, blk, fwd_ss, fwd_rs.at[p, j], sib_dev)

    def fwd_got(p, j):
        blk = panel.at[p, chip(-j), 1 - core]
        return remote(blk, blk, fwd_ss, fwd_rs.at[p, j], sib_dev)

    def send(p):
        loads[p].wait()

        @pl.loop(1, 8)
        def _(j):
            tok_copy(p, j).start()

        fwd_copy(p, 0).start()

    def forward(p):
        @pl.loop(1, 8)
        def _(j):
            tok_copy(p, j).wait_recv()
            fwd_copy(p, j).start()

    def gathered(p):
        @pl.loop(0, 8)
        def _(j):
            fwd_got(p, j).wait_recv()

    def partial(m, rows, col):
        if m == 2:
            return dot(rows, dw[pl.ds(col, TILE), :], 1, 1)
        return dot(rows, (gw, uw)[m][:, pl.ds(col, TILE)], 1, 0)

    def tile(i):
        return pl.ds(i * TILE, TILE)

    def part_a(ms, dst, x, f):
        for m in ms:
            rows = panel[m // 2, :, x].reshape(NZ * NB, 512)
            for i in range(na):
                dst[:, m, :, tile(i)] = f(partial(m, rows, i * TILE)).reshape(NZ, NB, TILE)

    def part_b(ms):
        for m in ms:
            rows = panel[m // 2].reshape(2 * NZ * NB, 512)
            for i in range(nb):
                v = partial(m, rows, wa + i * TILE).reshape(NZ, 2, NB, TILE)
                for x in range(2):
                    pb[:, 3 * x + m, :, tile(i)] = v[:, x]

    def xa_copy(k, g):
        d = zp(k)
        ms = (pl.ds(0, 2), pl.ds(2, 1))[g]
        return remote(xa_s.at[d, ms], xa_r.at[d, ms], xa_ss, xa_rs.at[g, d], x_dev)

    order = (4, 3, -3, 2, -2, 1, -1, 0)
    send(0)
    send(1)
    forward(0)
    gathered(0)
    loads[2].wait()
    loads[3].wait()
    part_a((0, 1), xa_s, xo, enc)
    for k in order[:2]:
        xa_copy(k, 0).start()
    part_b((0, 1))
    forward(1)
    gathered(1)
    loads[4].wait()
    part_b((2,))

    def hop(dst, own, recv, lo, hi):
        width = own.shape[-1] // 2

        @pl.loop(0, own.shape[0])
        def _(m):
            for i in range(lo, hi):
                c = pl.ds(i * width, width)
                v = own[m, :, c]
                for r in recv:
                    v = v + dec(r[m, :, c])
                dst[m, :, c] = enc(v) if dst.dtype == BF16 else v

    class Ring:
        def __init__(self, own, s, r, ss, rs):
            self.own, self.s, self.r, self.ss, self.rs = own, s, r, ss, rs
            self.half = s.shape[-1] // 2

        def copy(self, step, d):
            src, dst = self.s.at[d, step - 1], self.r.at[d, step - 1]
            if step == 1:
                c = pl.ds(d * self.half, self.half)
                src, dst = src.at[:, :, c], dst.at[:, :, c]
            return remote(src, dst, self.ss.at[min(step - 1, 1)], self.rs.at[d, step - 1], z_dev[d])

        def step(self, step):
            for d in range(2):
                own = self.own(zp((5 - step) * (-1, 1)[d]))
                src = self.s.at[d, step - 1]
                if step == 1:
                    hop(src, own, (), d, d + 1)
                else:
                    self.copy(step - 1, d).wait_recv()
                    got = self.r.at[d, step - 2]
                    if step == 2:
                        hop(src, own, (got,), d, d + 1)
                        hop(src, own, (), 1 - d, 2 - d)
                    else:
                        hop(src, own, (got,), 0, 2)
                self.copy(step, d).start()

        def finish(self, dst):
            for d in range(2):
                self.copy(4, d).wait_recv()
            hop(dst, self.own(z), (self.r.at[0, 3], self.r.at[1, 3]), 0, 2)

        def drain(self):
            one, rest = self.s.at[0, 0], self.s.at[:, pl.ds(1, 3)]
            remote(one, one, self.ss.at[0], self.rs.at[0, 0], z_dev[0]).wait_send()
            remote(rest, rest, self.ss.at[1], self.rs.at[0, 0], z_dev[0]).wait_send()

    ha = wa // 2
    cols_a = (pl.ds(0, ha), pl.ds(ha, ha))
    xs = (xo, xh)
    rings_a = [
        Ring(lambda d, c=cols_a[i]: pa.at[d, :, :, c], sa.at[i], ra.at[i], za_ss.at[i], za_rs.at[i]) for i in range(2)
    ]
    rings_b = [
        Ring(lambda d, x=xs[i]: pb.at[d, pl.ds(3 * x, 3)], sb.at[i], rb.at[i], zb_ss.at[i], zb_rs.at[i])
        for i in range(2)
    ]

    def step_a(step):
        for ring in rings_a:
            ring.step(step)

    def step_b(step):
        for ring in rings_b:
            ring.step(step)

    step_b(1)
    part_a((2,), xa_s, xo, enc)
    for k in order[:2]:
        xa_copy(k, 1).start()
    for k in order[2:]:
        for g in range(2):
            xa_copy(k, g).start()
    part_a((0, 1, 2), pa, xh, lambda v: v)

    def take_x(k):
        for g in range(2):
            xa_copy(k, g).wait_recv()
        d = zp(k)
        hop(pa.at[d], pa.at[d], (xa_r.at[d],), 0, 2)

    step_b(2)
    take_x(4)
    step_a(1)
    for s, ks in ((2, (3, -3)), (3, (2, -2))):
        step_b(s + 1)
        for k in ks:
            take_x(k)
        step_a(s)
    rings_b[0].finish(xb_s)
    xb_copy = remote(xb_s, xb_r, xb_ss, xb_rs, x_dev)
    xb_copy.start()
    for k in (1, -1):
        take_x(k)
    step_a(4)
    take_x(0)
    own_b = pb.at[z, pl.ds(3 * xh, 3)]
    rings_b[1].finish(own_b)

    def local(src, dst, n, base):
        for i in range(n):
            gate, up, cap_grad = src[0, :, tile(i)], src[1, :, tile(i)], src[2, :, tile(i)]
            at = 2 * (base + i)
            codes = jnp.concatenate([cap_in[at : at + 1, :], cap_in[at + 1 : at + 2, :]], axis=1)
            cap = codes.astype(F32) * (1.0 / 512.0)
            sig = 1.0 / (1.0 + jnp.exp(-gate))
            act = gate * sig
            squash = jnp.tanh(act * up / cap)
            hid_grad = cap_grad * (1.0 - squash * squash)
            dst[0, :, tile(i)] = (cap * squash).astype(BF16)
            dst[1, :, tile(i)] = (hid_grad * up * sig * (1.0 + gate * (1.0 - sig))).astype(BF16)
            dst[2, :, tile(i)] = (hid_grad * act).astype(BF16)

    xb_copy.wait()
    hop(own_b, own_b, (xb_r,), 0, 2)
    local(own_b, gb.at[z, pl.ds(3 * xh, 3)], nb, na)

    def gxb_copy(x):
        blk = gb.at[z, pl.ds(3 * x, 3)]
        return remote(blk, blk, gxb_ss, gxb_rs, x_dev)

    gxb_copy(xh).start()
    for i in range(2):
        rings_a[i].finish(pa.at[z, :, :, cols_a[i]])
    local(pa.at[z], ga.at[z, xh], na, 0)

    def halves(blk, step, d, width):
        return blk.at[:, :, pl.ds(d * (width // 2), width // 2)] if step == 4 else blk

    def gza_copy(i, step, d, got=False):
        blk = ga.at[zp((step if got else step - 1) * (1, -1)[d]), xh, :, :, cols_a[i]]
        blk = halves(blk, step, d, ha)
        return remote(blk, blk, gza_ss.at[step // 4], gza_rs.at[i, d, step - 1], z_dev[d])

    def gxa_copy(i, k, got=False):
        blk = ga.at[zp(k), xo if got else xh, :, :, cols_a[i]]
        return remote(blk, blk, gxa_ss, gxa_rs.at[i, zp(k)], x_dev)

    def gzb_copy(i, step, d, got=False):
        blk = gb.at[zp((step if got else step - 1) * (1, -1)[d]), pl.ds(3 * xs[i], 3)]
        blk = halves(blk, step, d, wb)
        return remote(blk, blk, gzb_ss.at[step // 4], gzb_rs.at[i, d, step - 1], z_dev[d])

    def keep_a(k, x):
        d = zp(k)
        t = pl.multiple_of((d * 2 + x) * NB, NB)
        return pltpu.make_async_copy(ga.at[d, x], d_out.at[:, pl.ds(t, NB), pl.ds(0, wa)], dsem.at[0])

    def keep_b(k, x):
        d = zp(k)
        t = pl.multiple_of((d * 2 + x) * NB, NB)
        return pltpu.make_async_copy(
            gb.at[d, pl.ds(3 * x, 3)], d_out.at[:, pl.ds(t, NB), pl.ds(wa, wb)], dsem.at[1]
        )

    def keep_bs(k):
        for x in range(2):
            keep_b(k, x).start()

    for i in range(2):
        for d in range(2):
            gza_copy(i, 1, d).start()
    for d in range(2):
        gzb_copy(1, 1, d).start()
    for i in range(2):
        gxa_copy(i, 0).start()
    keep_a(0, xh).start()
    keep_panel = pltpu.make_async_copy(panel, panel_out, lsem.at[0])
    keep_panel.start()

    def ig_rows(ks, a=True, b=True):
        def rows(ref):
            return jnp.concatenate([ref(zp(k), x) for k in ks for x in range(2)], axis=0)

        v = 0.0
        for m, wt in ((1, gw), (2, uw)):
            if a:
                v = v + dot(rows(lambda d, x: ga[d, x, m]), wt[:, :wa], 1, 1)
            if b:
                v = v + dot(rows(lambda d, x: gb[d, 3 * x + m]), wt[:, wa:], 1, 1)
        for n_k, k in enumerate(ks):
            part = v[n_k * 2 * NB : (n_k + 1) * 2 * NB].reshape(2, NB, 512)
            ig_acc[zp(k)] = part if a else ig_acc[zp(k)] + part
        if not b:
            return
        for k in ks:
            d = zp(k)
            sib_s[d] = ig_acc[d, 1 - core].astype(BF16)
            sib_copy(d).start()

    def ig_send(ks):
        for k in ks:
            d = zp(k)
            sib_copy(d).wait_recv()
            v = ig_acc[d, core] + sib_r[d].astype(F32)
            ig_acc[d, core] = v
            ig_s[d] = v.astype(BF16)

            @pl.when(d != q)
            def _():
                ig_copy((d - q + 8) % 8).start()

    def ig_copy(j):
        return remote(ig_s.at[chip(j)], ig_r.at[j], ig_ss, ig_rs.at[j], peer(j))

    def sib_copy(d):
        return remote(sib_s.at[d], sib_r.at[d], sib_ss, sib_rs.at[d], sib_dev)

    def take_gx(k):
        for i in range(2):
            gxa_copy(i, k, True).wait_recv()
        keep_a(k, xo).start()

    def forward_a(step):
        for i in range(2):
            for d in range(2):
                k = (step - 1) * (1, -1)[d]
                gza_copy(i, step - 1, d, True).wait_recv()
                gza_copy(i, step, d).start()
                gxa_copy(i, k).start()
                if i == 1:
                    keep_a(k, xh).start()

    def forward_b(i, step):
        for d in range(2):
            gzb_copy(i, step - 1, d, True).wait_recv()
            gzb_copy(i, step, d).start()
            keep_b((step - 1) * (1, -1)[d], xs[i]).start()

    forward_a(2)
    gxb_copy(xo).wait_recv()
    for d in range(2):
        gzb_copy(0, 1, d).start()
    keep_bs(0)
    forward_b(1, 2)
    forward_a(3)
    forward_b(0, 2)
    forward_a(4)
    forward_b(1, 3)
    forward_b(0, 3)

    def sent(ref, sem):
        remote(ref, ref, sem, gxb_rs, x_dev).wait_send()

    sent(panel.at[0, pl.ds(0, 7)], tok_ss)
    sent(panel.at[0], fwd_ss)
    sent(xa_s, xa_ss)
    for ring in rings_a + rings_b:
        ring.drain()
    early = (0, 1, -1, 2, -2)
    for k in early:
        take_gx(k)
    ig_rows(early)
    for i in range(2):
        for d in range(2):
            gza_copy(i, 4, d, True).wait_recv()
        gxa_copy(i, 4).start()
    keep_a(4, xh).start()
    forward_b(1, 4)
    forward_b(0, 4)
    ig_send(early)
    for k in (3, -3):
        take_gx(k)
    ig_rows((3, -3))
    ig_send((3, -3))
    take_gx(4)
    ig_rows((4,), b=False)
    for i in (1, 0):
        for d in range(2):
            gzb_copy(i, 4, d, True).wait_recv()
    keep_bs(4)
    ig_rows((4,), a=False)
    ig_send((4,))

    sent(xa_s, gxa_ss)
    sent(sib_s, sib_ss)
    sent(sa.at[:, 0, 0], gza_ss.at[1])
    sent(sa.at[:, :, pl.ds(0, 3)], gza_ss.at[0])
    sent(sb.at[:, 0, 0], gzb_ss.at[1])
    sent(sb.at[:, :, pl.ds(0, 3)], gzb_ss.at[0])
    gxb_copy(xh).wait_send()

    @pl.loop(1, 8)
    def _(j):
        ig_copy(j).wait_recv()
        ig_acc[q, core] += ig_r[j].astype(F32)

    sent(ig_s.at[pl.ds(0, 7)], ig_ss)
    last = pltpu.make_async_copy(ig_acc.at[q, core], ig_out, lsem.at[1])
    last.start()

    pltpu.make_async_copy(ga, ga, dsem.at[0]).wait()
    pltpu.make_async_copy(gb, gb, dsem.at[1]).wait()
    keep_panel.wait()
    last.wait()


def weight_grads(
    d_in, panel_in, ig_in, ig_out, gg_out, ug_out, dg_out, d, panel, gg, ug, dg, ig_v, ig_b, isem, osem
):
    first, rest = pl.ds(0, 2 * TILE), pl.ds(2 * TILE, d.shape[2] - 2 * TILE)
    loads = []
    for src, dst in (
        (panel_in.at[0], panel.at[0]),
        (d_in.at[1, :, first], d.at[1, :, first]),
        (d_in.at[1, :, rest], d.at[1, :, rest]),
        (d_in.at[2], d.at[2]),
        (panel_in.at[1], panel.at[1]),
        (d_in.at[0], d.at[0]),
        (ig_in, ig_v),
    ):
        loads.append(pltpu.make_async_copy(src, dst, isem.at[len(loads)]))
        loads[-1].start()
    n = d.shape[2] // TILE
    stores = []

    def store(src, dst):
        stores.append(pltpu.make_async_copy(src, dst, osem.at[len(stores)]))
        stores[-1].start()

    loads[0].wait()
    loads[1].wait()
    for m, dst, out in ((1, gg, gg_out), (2, ug, ug_out)):
        for i in range(n):
            if (m, i) == (1, 2):
                loads[2].wait()
            if (m, i) == (2, 0):
                loads[3].wait()
            c = pl.ds(i * TILE, TILE)
            dst[:, c] = dot(panel[0], d[m, :, c], 0, 0).astype(BF16)
        store(dst, out)
    loads[6].wait()
    ig_b[...] = ig_v[...].astype(BF16)
    store(ig_b, ig_out)
    loads[4].wait()
    loads[5].wait()
    for lo, hi in ((0, 4), (4, 6), (6, 7)):
        for i in range(lo, hi):
            c = pl.ds(i * TILE, TILE)
            dg[c, :] = dot(d[0, :, c], panel[1], 0, 0).astype(BF16)
        rows = pl.ds(lo * TILE, (hi - lo) * TILE)
        store(dg.at[rows], dg_out.at[rows])
    for c in stores:
        c.wait()


def per_device(tokens, out_grad, gate_weight, up_weight, down_weight, cap_codes):
    hidden = gate_weight.shape[1]
    n = hidden // TILE
    na = 4
    nb = n - na
    wa, wb = na * TILE, nb * TILE
    dma = pltpu.SemaphoreType.DMA
    sh = jax.ShapeDtypeStruct
    scratch = [
        pltpu.VMEM((512, hidden), BF16),
        pltpu.VMEM((512, hidden), BF16),
        pltpu.VMEM((hidden, 512), BF16),
        pltpu.VMEM((2, NZ, 2, NB, 512), BF16),
        pltpu.VMEM((NZ, 3, NB, wa), F32),
        pltpu.VMEM((NZ, 6, NB, wb), F32),
        pltpu.VMEM((NZ, 3, NB, wa), BF16),
        pltpu.VMEM((NZ, 3, NB, wa), BF16),
        pltpu.VMEM((2, 2, 4, 3, NB, wa // 2), BF16),
        pltpu.VMEM((2, 2, 4, 3, NB, wa // 2), BF16),
        pltpu.VMEM((2, 2, 4, 3, NB, wb), BF16),
        pltpu.VMEM((2, 2, 4, 3, NB, wb), BF16),
        pltpu.VMEM((3, NB, wb), BF16),
        pltpu.VMEM((3, NB, wb), BF16),
        pltpu.VMEM((NZ, 2, 3, NB, wa), BF16),
        pltpu.VMEM((NZ, 6, NB, wb), BF16),
        pltpu.VMEM((NZ, 2, NB, 512), F32),
        pltpu.VMEM((NZ, NB, 512), BF16),
        pltpu.VMEM((NZ, NB, 512), BF16),
        pltpu.VMEM((NZ, NB, 512), BF16),
        pltpu.VMEM((NZ, NB, 512), BF16),
        dma((5,)), dma((2,)),
        dma, dma((2, 8)),
        dma, dma((2, 8)),
        dma, dma((2, NZ)),
        dma((2, 2)), dma((2, 2, 4)),
        dma((2, 2)), dma((2, 2, 4)),
        dma, dma,
        dma, dma((2, NZ)),
        dma((2,)), dma((2, 2, 4)),
        dma((2,)), dma((2, 2, 4)),
        dma, dma,
        dma, dma((NZ,)),
        dma, dma((NZ,)),
    ]
    any_spec = pl.BlockSpec(memory_space=pl.ANY)
    deltas, panel, ig_sum = pl.pallas_call(
        functools.partial(kernel, na, nb),
        out_shape=(sh((3, 512, hidden), BF16), sh((2, NZ, 2, NB, 512), BF16), sh((NB, 512), F32)),
        in_specs=[any_spec] * 5 + [pl.BlockSpec(memory_space=pltpu.VMEM)],
        out_specs=[any_spec] * 3,
        scratch_shapes=scratch,
        compiler_params=pltpu.CompilerParams(
            collective_id=0, has_side_effects=True, vmem_limit_bytes=60 << 20
        ),
        name="exchange",
    )(tokens, out_grad, gate_weight, up_weight, down_weight, cap_codes.reshape(hidden // 128, 128))
    return pl.pallas_call(
        weight_grads,
        out_shape=(
            sh((NB, 512), BF16),
            sh((512, hidden), BF16),
            sh((512, hidden), BF16),
            sh((hidden, 512), BF16),
        ),
        in_specs=[any_spec] * 3,
        out_specs=(any_spec,) * 4,
        scratch_shapes=[
            pltpu.VMEM((3, 512, hidden), BF16),
            pltpu.VMEM((2, 512, 512), BF16),
            pltpu.VMEM((512, hidden), BF16),
            pltpu.VMEM((512, hidden), BF16),
            pltpu.VMEM((hidden, 512), BF16),
            pltpu.VMEM((NB, 512), F32),
            pltpu.VMEM((NB, 512), BF16),
            dma((7,)),
            dma((6,)),
        ],
        compiler_params=pltpu.CompilerParams(vmem_limit_bytes=60 << 20),
        name="weight_grads",
    )(deltas, panel.reshape(2, 512, 512), ig_sum)


def solution(mesh):
    return jax.shard_map(
        per_device,
        mesh=mesh,
        in_specs=(
            P("hid", "wid"),
            P("hid", "wid"),
            P("wid", "hid"),
            P("wid", "hid"),
            P("hid", "wid"),
            P("hid"),
        ),
        out_specs=(P("hid", "wid"), P("wid", "hid"), P("wid", "hid"), P("hid", "wid")),
        check_vma=False,
    )
```

```python
import functools

import jax
import jax.numpy as jnp
from jax import lax
from jax.experimental import pallas as pl
from jax.experimental.pallas import tpu as pltpu
from jax.sharding import PartitionSpec as P

MESH = pl.DeviceIdType.MESH
BF16 = jnp.bfloat16
F32 = jnp.float32

TILE = 256
NB = 32
NZ = 8
SCALE = 2.0**18


def dot(a, b, ca, cb):
    return lax.dot_general(a, b, (((ca,), (cb,)), ((), ())), preferred_element_type=F32)


def enc(v):
    u = v * SCALE
    return ((u * jnp.abs(u)) * (u * u)).astype(BF16)


def dec(y):
    y = y.astype(F32)
    root = lax.rsqrt(lax.rsqrt(jnp.maximum(jnp.abs(y), 2e-38)))
    return root * jnp.where(y < 0.0, -1.0 / SCALE, 1.0 / SCALE)


def kernel(
    na, nb,
    tok_in, og_in, gw_in, uw_in, dw_in, cap_in,
    d_out, panel_out, ig_out,
    gw, uw, dw, panel,
    pa, pb, xa_s, xa_r, sa, ra, sb, rb, xb_s, xb_r,
    ga, gb, ig_acc, sib_s, sib_r, ig_s,
    lsem, dsem, tok_ss, tok_rs, fwd_ss, fwd_rs, xa_ss, xa_rs, za_ss, za_rs, zb_ss, zb_rs, xb_ss, xb_rs,
    gxa_ss, gxa_rs, gza_ss, gza_rs, gzb_ss, gzb_rs, gxb_ss, gxb_rs, sib_ss, sib_rs, ig_ss, ig_rs,
):
    wa, wb = na * TILE, nb * TILE
    h, w = lax.axis_index("hid"), lax.axis_index("wid")
    z, xh = w // 2, w % 2
    xo = 1 - xh
    q, core = h // 2, h % 2
    zp = lambda k: (z + k + NZ) % NZ
    up_dev, dn_dev, x_dev = (h, zp(1) * 2 + xh), (h, zp(-1) * 2 + xh), (h, z * 2 + xo)
    z_dev = (dn_dev, up_dev)
    sib_dev = (q * 2 + 1 - core, w)
    chip = lambda j: (q + j + 8) % 8
    peer = lambda j: (chip(j) * 2 + core, w)

    def remote(src, dst, ss, rs, dev):
        return pltpu.make_async_remote_copy(
            src_ref=src, dst_ref=dst, send_sem=ss, recv_sem=rs, device_id=dev, device_id_type=MESH
        )

    loads = [
        pltpu.make_async_copy(tok_in, panel.at[0, q, core], lsem.at[0]),
        pltpu.make_async_copy(og_in, panel.at[1, q, core], lsem.at[1]),
        pltpu.make_async_copy(gw_in, gw, lsem.at[2]),
        pltpu.make_async_copy(uw_in, uw, lsem.at[3]),
        pltpu.make_async_copy(dw_in, dw, lsem.at[4]),
    ]
    for c in loads:
        c.start()

    bar = pltpu.get_barrier_semaphore()
    for dev in (up_dev, dn_dev, x_dev, sib_dev):
        pl.semaphore_signal(bar, inc=1, device_id=dev, device_id_type=MESH)
    for j in range(1, 8):
        pl.semaphore_signal(bar, inc=1, device_id=peer(j), device_id_type=MESH)
    pl.semaphore_wait(bar, 11)

    def tok_copy(p, j):
        mine = panel.at[p, q, core]
        return remote(mine, mine, tok_ss, tok_rs.at[p, j], peer(j))

    def fwd_copy(p, j):
        blk = panel.at[p, chip(-j), core]
        return remote(blk, blk, fwd_ss, fwd_rs.at[p], sib_dev)

    def fwd_got(p, j):
        blk = panel.at[p, chip(-j), 1 - core]
        return remote(blk, blk, fwd_ss, fwd_rs.at[p], sib_dev)

    def send(p):
        loads[p].wait()

        @pl.loop(1, 8)
        def _(j):
            tok_copy(p, j).start()

        fwd_copy(p, 0).start()

    def forward(p, lo=1, hi=8):
        @pl.loop(lo, hi)
        def _(j):
            tok_copy(p, j).wait_recv()
            fwd_copy(p, j).start()

    def gathered(p):
        half = panel.at[p, pl.ds(0, 4)]
        remote(half, half, fwd_ss, fwd_rs.at[p], sib_dev).wait_recv()

    def partial(m, rows, col):
        if m == 2:
            return dot(rows, dw[pl.ds(col, TILE), :], 1, 1)
        return dot(rows, (gw, uw)[m][:, pl.ds(col, TILE)], 1, 0)

    def tile(i):
        return pl.ds(i * TILE, TILE)

    def part_a(ms, dst, x, f):
        for m in ms:
            rows = panel[m // 2, :, x].reshape(NZ * NB, 512)
            for i in range(na):
                dst[:, m, :, tile(i)] = f(partial(m, rows, i * TILE)).reshape(NZ, NB, TILE)

    def part_b(ms):
        for m in ms:
            rows = panel[m // 2].reshape(2 * NZ * NB, 512)
            for i in range(nb):
                v = partial(m, rows, wa + i * TILE).reshape(NZ, 2, NB, TILE)
                for x in range(2):
                    pb[:, 3 * x + m, :, tile(i)] = v[:, x]

    def xa_copy(k, g):
        d = zp(k)
        ms = (pl.ds(0, 2), pl.ds(2, 1))[g]
        return remote(xa_s.at[d, ms], xa_r.at[d, ms], xa_ss, xa_rs.at[g, d], x_dev)

    def hop(dst, own, recv, lo, hi, m0=0, m1=3):
        width = own.shape[-1] // 2

        @pl.loop(m0, m1)
        def _(m):
            for i in range(lo, hi):
                c = pl.ds(i * width, width)
                v = own[m, :, c]
                for r in recv:
                    v = v + dec(r[m, :, c])
                dst[m, :, c] = enc(v) if dst.dtype == BF16 else v

    class Ring:
        def __init__(self, own, s, r, ss, rs):
            self.own, self.s, self.r, self.ss, self.rs = own, s, r, ss, rs
            self.half = s.shape[-1] // 2

        def copy(self, step, d):
            return self.copies(step, d, 0, 3, step - 1)

        def copies(self, step, d, m0, m1, sem):
            ms = pl.ds(m0, m1 - m0)
            src, dst = self.s.at[d, step - 1, ms], self.r.at[d, step - 1, ms]
            if step == 1:
                c = pl.ds(d * self.half, self.half)
                src, dst = src.at[:, :, c], dst.at[:, :, c]
            return remote(src, dst, self.ss.at[min(step - 1, 1)], self.rs.at[d, sem], z_dev[d])

        def first(self, m0, m1, sem):
            for d in range(2):
                own = self.own(zp(4 * (-1, 1)[d]))
                hop(self.s.at[d, 0], own, (), d, d + 1, m0, m1)
                self.copies(1, d, m0, m1, sem).start()

        def second(self, m0, m1, sem):
            for d in range(2):
                own, src, got = self.own(zp(3 * (-1, 1)[d])), self.s.at[d, 1], self.r.at[d, 0]
                self.copies(1, d, m0, m1, sem).wait_recv()
                hop(src, own, (got,), d, d + 1, m0, m1)
                hop(src, own, (), 1 - d, 2 - d, m0, m1)
                self.copies(2, d, m0, m1, sem + 1).start()

        def step(self, step, split=False):
            for d in range(2):
                own = self.own(zp((5 - step) * (-1, 1)[d]))
                src = self.s.at[d, step - 1]
                if step == 1:
                    hop(src, own, (), d, d + 1)
                else:
                    if split:
                        self.copies(step - 1, d, 0, 2, step - 2).wait_recv()
                        self.copies(step - 1, d, 2, 3, step + 2).wait_recv()
                    else:
                        self.copy(step - 1, d).wait_recv()
                    got = self.r.at[d, step - 2]
                    if step == 2:
                        hop(src, own, (got,), d, d + 1)
                        hop(src, own, (), 1 - d, 2 - d)
                    else:
                        hop(src, own, (got,), 0, 2)
                self.copy(step, d).start()

        def finish(self, dst):
            for d in range(2):
                self.copy(4, d).wait_recv()
            hop(dst, self.own(z), (self.r.at[0, 3], self.r.at[1, 3]), 0, 2)

        def drain(self):
            one, rest = self.s.at[0, 0], self.s.at[:, pl.ds(1, 3)]
            remote(one, one, self.ss.at[0], self.rs.at[0, 0], z_dev[0]).wait_send()
            remote(rest, rest, self.ss.at[1], self.rs.at[0, 0], z_dev[0]).wait_send()

    ha = wa // 2
    cols_a = (pl.ds(0, ha), pl.ds(ha, ha))
    xs = (xo, xh)
    rings_a = [
        Ring(lambda d, c=cols_a[i]: pa.at[d, :, :, c], sa.at[i], ra.at[i], za_ss.at[i], za_rs.at[i]) for i in range(2)
    ]
    rings_b = [
        Ring(lambda d, x=xs[i]: pb.at[d, pl.ds(3 * x, 3)], sb.at[i], rb.at[i], zb_ss.at[i], zb_rs.at[i])
        for i in range(2)
    ]

    def step_a(step):
        for ring in rings_a:
            ring.step(step)

    def step_b(step):
        for ring in rings_b:
            ring.step(step, split=step == 3)

    order = (4, 3, -3, 2, -2, 1, -1, 0)
    send(0)
    send(1)
    forward(0)
    gathered(0)
    loads[2].wait()
    loads[3].wait()
    part_a((0, 1), xa_s, xo, enc)
    for k in order[:2]:
        xa_copy(k, 0).start()
    forward(1, 1, 5)
    part_b((0, 1))
    for ring in rings_b:
        ring.first(0, 2, 0)
    forward(1, 5)
    gathered(1)
    loads[4].wait()
    part_b((2,))
    for ring in rings_b:
        ring.first(2, 3, 4)
    part_a((2,), xa_s, xo, enc)
    for k in order[:2]:
        xa_copy(k, 1).start()
    for k in order[2:]:
        for g in range(2):
            xa_copy(k, g).start()
    for ring in rings_b:
        ring.second(0, 2, 0)
    part_a((0, 1, 2), pa, xh, lambda v: v)

    def take_x(k):
        for g in range(2):
            xa_copy(k, g).wait_recv()
        d = zp(k)
        hop(pa.at[d], pa.at[d], (xa_r.at[d],), 0, 2)

    for ring in rings_b:
        ring.second(2, 3, 4)
    take_x(4)
    step_a(1)
    for s, ks in ((2, (3, -3)), (3, (2, -2))):
        step_b(s + 1)
        for k in ks:
            take_x(k)
        step_a(s)
    rings_b[0].finish(xb_s)
    xb_copy = remote(xb_s, xb_r, xb_ss, xb_rs, x_dev)
    xb_copy.start()
    for k in (1, -1):
        take_x(k)
    step_a(4)
    take_x(0)
    own_b = pb.at[z, pl.ds(3 * xh, 3)]
    rings_b[1].finish(own_b)

    def local(src, dst, n, base):
        for i in range(n):
            gate, up, cap_grad = src[0, :, tile(i)], src[1, :, tile(i)], src[2, :, tile(i)]
            at = 2 * (base + i)
            codes = jnp.concatenate([cap_in[at : at + 1, :], cap_in[at + 1 : at + 2, :]], axis=1)
            cap = codes.astype(F32) * (1.0 / 512.0)
            sig = 1.0 / (1.0 + jnp.exp(-gate))
            act = gate * sig
            squash = jnp.tanh(act * up / cap)
            hid_grad = cap_grad * (1.0 - squash * squash)
            dst[0, :, tile(i)] = (cap * squash).astype(BF16)
            dst[1, :, tile(i)] = (hid_grad * up * sig * (1.0 + gate * (1.0 - sig))).astype(BF16)
            dst[2, :, tile(i)] = (hid_grad * act).astype(BF16)

    def halves(blk, step, d, width):
        return blk.at[:, :, pl.ds(d * (width // 2), width // 2)] if step == 4 else blk

    def gza_copy(i, step, d, got=False):
        blk = ga.at[zp((step if got else step - 1) * (1, -1)[d]), xh, :, :, cols_a[i]]
        blk = halves(blk, step, d, ha)
        return remote(blk, blk, gza_ss.at[step // 4], gza_rs.at[i, d, step - 1], z_dev[d])

    def gxa_copy(i, k, got=False):
        blk = ga.at[zp(k), xo if got else xh, :, :, cols_a[i]]
        return remote(blk, blk, gxa_ss, gxa_rs.at[i, zp(k)], x_dev)

    def gzb_copy(i, step, d, got=False):
        blk = gb.at[zp((step if got else step - 1) * (1, -1)[d]), pl.ds(3 * xs[i], 3)]
        blk = halves(blk, step, d, wb)
        return remote(blk, blk, gzb_ss.at[step // 4], gzb_rs.at[i, d, step - 1], z_dev[d])

    xb_copy.wait()
    hop(own_b, own_b, (xb_r,), 0, 2)
    local(own_b, gb.at[z, pl.ds(3 * xh, 3)], nb, na)

    def gxb_copy(x):
        blk = gb.at[z, pl.ds(3 * x, 3)]
        return remote(blk, blk, gxb_ss, gxb_rs, x_dev)

    gxb_copy(xh).start()
    for d in range(2):
        gzb_copy(1, 1, d).start()
    for i in range(2):
        rings_a[i].finish(pa.at[z, :, :, cols_a[i]])
    local(pa.at[z], ga.at[z, xh], na, 0)

    def keep_a(k, x):
        d = zp(k)
        t = pl.multiple_of((d * 2 + x) * NB, NB)
        return pltpu.make_async_copy(ga.at[d, x], d_out.at[:, pl.ds(t, NB), pl.ds(0, wa)], dsem.at[0])

    def keep_b(k, x):
        d = zp(k)
        t = pl.multiple_of((d * 2 + x) * NB, NB)
        return pltpu.make_async_copy(
            gb.at[d, pl.ds(3 * x, 3)], d_out.at[:, pl.ds(t, NB), pl.ds(wa, wb)], dsem.at[1]
        )

    def keep_bs(k):
        for x in range(2):
            keep_b(k, x).start()

    for i in range(2):
        for d in range(2):
            gza_copy(i, 1, d).start()
    for i in range(2):
        gxa_copy(i, 0).start()
    keep_a(0, xh).start()
    keep_panel = pltpu.make_async_copy(panel, panel_out, lsem.at[0])
    keep_panel.start()

    def ig_rows(ks, a=True, b=True):
        def rows(ref):
            return jnp.concatenate([ref(zp(k), x) for k in ks for x in range(2)], axis=0)

        v = 0.0
        for m, wt in ((1, gw), (2, uw)):
            if a:
                v = v + dot(rows(lambda d, x: ga[d, x, m]), wt[:, :wa], 1, 1)
            if b:
                v = v + dot(rows(lambda d, x: gb[d, 3 * x + m]), wt[:, wa:], 1, 1)
        for n_k, k in enumerate(ks):
            part = v[n_k * 2 * NB : (n_k + 1) * 2 * NB].reshape(2, NB, 512)
            ig_acc[zp(k)] = part if a else ig_acc[zp(k)] + part
        if not b:
            return
        for k in ks:
            d = zp(k)
            sib_s[d] = ig_acc[d, 1 - core].astype(BF16)
            sib_copy(d).start()

    def ig_send(ks):
        for k in ks:
            d = zp(k)
            sib_copy(d).wait_recv()
            ig_s[d] = (ig_acc[d, core] + sib_r[d].astype(F32)).astype(BF16)

            @pl.when(d != q)
            def _():
                ig_copy((d - q + 8) % 8).start()

    def ig_copy(j):
        return remote(ig_s.at[chip(j)], ig_out.at[j], ig_ss, ig_rs, peer(j))

    def sib_copy(d):
        return remote(sib_s.at[d], sib_r.at[d], sib_ss, sib_rs.at[d], sib_dev)

    def take_gx(k):
        for i in range(2):
            gxa_copy(i, k, True).wait_recv()
        keep_a(k, xo).start()

    def forward_a(step):
        for i in range(2):
            for d in range(2):
                k = (step - 1) * (1, -1)[d]
                gza_copy(i, step - 1, d, True).wait_recv()
                gza_copy(i, step, d).start()
                gxa_copy(i, k).start()
                if i == 1:
                    keep_a(k, xh).start()

    def forward_b(i, step):
        for d in range(2):
            gzb_copy(i, step - 1, d, True).wait_recv()
            gzb_copy(i, step, d).start()
            keep_b((step - 1) * (1, -1)[d], xs[i]).start()

    forward_a(2)
    gxb_copy(xo).wait_recv()
    for d in range(2):
        gzb_copy(0, 1, d).start()
    keep_bs(0)
    forward_b(1, 2)
    forward_a(3)
    forward_b(0, 2)
    forward_a(4)
    forward_b(1, 3)
    forward_b(0, 3)

    def sent(ref, sem):
        remote(ref, ref, sem, gxb_rs, x_dev).wait_send()

    sent(panel.at[0, pl.ds(0, 7)], tok_ss)
    sent(panel.at[0], fwd_ss)
    sent(xa_s, xa_ss)
    for ring in rings_a + rings_b:
        ring.drain()
    early = (0, 1, -1, 2, -2)
    for k in early:
        take_gx(k)
    ig_rows(early)
    for i in range(2):
        for d in range(2):
            gza_copy(i, 4, d, True).wait_recv()
        gxa_copy(i, 4).start()
    keep_a(4, xh).start()
    forward_b(1, 4)
    forward_b(0, 4)
    ig_send(early)
    for k in (3, -3):
        take_gx(k)
    ig_rows((3, -3))
    ig_send((3, -3))
    take_gx(4)
    ig_rows((4,), b=False)
    for i in (1, 0):
        for d in range(2):
            gzb_copy(i, 4, d, True).wait_recv()
    keep_bs(4)
    ig_rows((4,), a=False)
    ig_send((4,))
    last = pltpu.make_async_copy(ig_s.at[q], ig_out.at[0], lsem.at[1])
    last.start()

    sent(xa_s, gxa_ss)
    sent(sib_s, sib_ss)
    sent(sa.at[:, 0, 0], gza_ss.at[1])
    sent(sa.at[:, :, pl.ds(0, 3)], gza_ss.at[0])
    sent(sb.at[:, 0, 0], gzb_ss.at[1])
    sent(sb.at[:, :, pl.ds(0, 3)], gzb_ss.at[0])
    gxb_copy(xh).wait_send()

    pieces = pl.ds(0, 7)
    remote(ig_s.at[pieces], ig_out.at[pl.ds(1, 7)], ig_ss, ig_rs, x_dev).wait()
    pltpu.make_async_copy(ga, ga, dsem.at[0]).wait()
    pltpu.make_async_copy(gb, gb, dsem.at[1]).wait()
    keep_panel.wait()
    last.wait()


def weight_grads(
    d_in, panel_in, ig_in, ig_out, gg_out, ug_out, dg_out, d, panel, gg, ug, dg, ig_v, ig_b, isem, osem
):
    first, rest = pl.ds(0, 2 * TILE), pl.ds(2 * TILE, d.shape[2] - 2 * TILE)
    loads = []
    for src, dst in (
        (panel_in.at[0], panel.at[0]),
        (d_in.at[1, :, first], d.at[1, :, first]),
        (d_in.at[1, :, rest], d.at[1, :, rest]),
        (d_in.at[2], d.at[2]),
        (panel_in.at[1], panel.at[1]),
        (d_in.at[0], d.at[0]),
        (ig_in, ig_v),
    ):
        loads.append(pltpu.make_async_copy(src, dst, isem.at[len(loads)]))
        loads[-1].start()
    n = d.shape[2] // TILE
    stores = []

    def store(src, dst):
        stores.append(pltpu.make_async_copy(src, dst, osem.at[len(stores)]))
        stores[-1].start()

    loads[0].wait()
    loads[1].wait()
    for m, dst, out in ((1, gg, gg_out), (2, ug, ug_out)):
        for i in range(n):
            if (m, i) == (1, 2):
                loads[2].wait()
            if (m, i) == (2, 0):
                loads[3].wait()
            c = pl.ds(i * TILE, TILE)
            dst[:, c] = dot(panel[0], d[m, :, c], 0, 0).astype(BF16)
        store(dst, out)
    loads[6].wait()
    ig_b[...] = sum(ig_v[j].astype(F32) for j in range(8)).astype(BF16)
    store(ig_b, ig_out)
    loads[4].wait()
    loads[5].wait()
    for lo, hi in ((0, 4), (4, 6), (6, 7)):
        for i in range(lo, hi):
            c = pl.ds(i * TILE, TILE)
            dg[c, :] = dot(d[0, :, c], panel[1], 0, 0).astype(BF16)
        rows = pl.ds(lo * TILE, (hi - lo) * TILE)
        store(dg.at[rows], dg_out.at[rows])
    for c in stores:
        c.wait()


def per_device(tokens, out_grad, gate_weight, up_weight, down_weight, cap_codes):
    hidden = gate_weight.shape[1]
    n = hidden // TILE
    na = 4
    nb = n - na
    wa, wb = na * TILE, nb * TILE
    dma = pltpu.SemaphoreType.DMA
    sh = jax.ShapeDtypeStruct
    scratch = [
        pltpu.VMEM((512, hidden), BF16),
        pltpu.VMEM((512, hidden), BF16),
        pltpu.VMEM((hidden, 512), BF16),
        pltpu.VMEM((2, NZ, 2, NB, 512), BF16),
        pltpu.VMEM((NZ, 3, NB, wa), F32),
        pltpu.VMEM((NZ, 6, NB, wb), F32),
        pltpu.VMEM((NZ, 3, NB, wa), BF16),
        pltpu.VMEM((NZ, 3, NB, wa), BF16),
        pltpu.VMEM((2, 2, 4, 3, NB, wa // 2), BF16),
        pltpu.VMEM((2, 2, 4, 3, NB, wa // 2), BF16),
        pltpu.VMEM((2, 2, 4, 3, NB, wb), BF16),
        pltpu.VMEM((2, 2, 4, 3, NB, wb), BF16),
        pltpu.VMEM((3, NB, wb), BF16),
        pltpu.VMEM((3, NB, wb), BF16),
        pltpu.VMEM((NZ, 2, 3, NB, wa), BF16),
        pltpu.VMEM((NZ, 6, NB, wb), BF16),
        pltpu.VMEM((NZ, 2, NB, 512), F32),
        pltpu.VMEM((NZ, NB, 512), BF16),
        pltpu.VMEM((NZ, NB, 512), BF16),
        pltpu.VMEM((NZ, NB, 512), BF16),
        dma((5,)), dma((2,)),
        dma, dma((2, 8)),
        dma, dma((2,)),
        dma, dma((2, NZ)),
        dma((2, 2)), dma((2, 2, 4)),
        dma((2, 2)), dma((2, 2, 6)),
        dma, dma,
        dma, dma((2, NZ)),
        dma((2,)), dma((2, 2, 4)),
        dma((2,)), dma((2, 2, 4)),
        dma, dma,
        dma, dma((NZ,)),
        dma, dma,
    ]
    any_spec = pl.BlockSpec(memory_space=pl.ANY)
    deltas, panel, ig_sum = pl.pallas_call(
        functools.partial(kernel, na, nb),
        out_shape=(sh((3, 512, hidden), BF16), sh((2, NZ, 2, NB, 512), BF16), sh((8, NB, 512), BF16)),
        in_specs=[any_spec] * 5 + [pl.BlockSpec(memory_space=pltpu.VMEM)],
        out_specs=[any_spec] * 3,
        scratch_shapes=scratch,
        compiler_params=pltpu.CompilerParams(
            collective_id=0, has_side_effects=True, vmem_limit_bytes=60 << 20
        ),
        name="exchange",
    )(tokens, out_grad, gate_weight, up_weight, down_weight, cap_codes.reshape(hidden // 128, 128))
    return pl.pallas_call(
        weight_grads,
        out_shape=(
            sh((NB, 512), BF16),
            sh((512, hidden), BF16),
            sh((512, hidden), BF16),
            sh((hidden, 512), BF16),
        ),
        in_specs=[any_spec] * 3,
        out_specs=(any_spec,) * 4,
        scratch_shapes=[
            pltpu.VMEM((3, 512, hidden), BF16),
            pltpu.VMEM((2, 512, 512), BF16),
            pltpu.VMEM((512, hidden), BF16),
            pltpu.VMEM((512, hidden), BF16),
            pltpu.VMEM((hidden, 512), BF16),
            pltpu.VMEM((8, NB, 512), BF16),
            pltpu.VMEM((NB, 512), BF16),
            dma((7,)),
            dma((6,)),
        ],
        compiler_params=pltpu.CompilerParams(vmem_limit_bytes=60 << 20),
        name="weight_grads",
    )(deltas, panel.reshape(2, 512, 512), ig_sum)


def solution(mesh):
    return jax.shard_map(
        per_device,
        mesh=mesh,
        in_specs=(
            P("hid", "wid"),
            P("hid", "wid"),
            P("wid", "hid"),
            P("wid", "hid"),
            P("hid", "wid"),
            P("hid"),
        ),
        out_specs=(P("hid", "wid"), P("wid", "hid"), P("wid", "hid"), P("hid", "wid")),
        check_vma=False,
    )
```

```python
import functools

import jax
import jax.numpy as jnp
from jax import lax
from jax.experimental import pallas as pl
from jax.experimental.pallas import tpu as pltpu
from jax.sharding import PartitionSpec as P

MESH = pl.DeviceIdType.MESH
BF16 = jnp.bfloat16
F32 = jnp.float32

TILE = 256
NB = 32
NZ = 8
SCALE = 2.0**18


def dot(a, b, ca, cb):
    return lax.dot_general(a, b, (((ca,), (cb,)), ((), ())), preferred_element_type=F32)


def enc(v):
    u = v * SCALE
    return ((u * jnp.abs(u)) * (u * u)).astype(BF16)


def dec(y):
    y = y.astype(F32)
    root = lax.rsqrt(lax.rsqrt(jnp.maximum(jnp.abs(y), 2e-38)))
    return root * jnp.where(y < 0.0, -1.0 / SCALE, 1.0 / SCALE)


def kernel(
    na, nb,
    tok_in, og_in, gw_in, uw_in, dw_in, cap_hbm,
    d_out, panel_out, ig_out,
    gw, uw, dw, panel, cap_in,
    pa, pb, xa_s, xa_r, sa, ra, sb, rb, xb_s, xb_r,
    ga, gb, ig_acc, sib_s, sib_r, ig_s,
    lsem, dsem, tok_ss, tok_rs, fwd_ss, fwd_rs, xa_ss, xa_rs, za_ss, za_rs, zb_ss, zb_rs, xb_ss, xb_rs,
    gxa_ss, gxa_rs, gza_ss, gza_rs, gzb_ss, gzb_rs, gxb_ss, gxb_rs, sib_ss, sib_rs, ig_ss, ig_rs,
):
    wa, wb = na * TILE, nb * TILE
    h, w = lax.axis_index("hid"), lax.axis_index("wid")
    z, xh = w // 2, w % 2
    xo = 1 - xh
    q, core = h // 2, h % 2
    zp = lambda k: (z + k + NZ) % NZ
    up_dev, dn_dev, x_dev = (h, zp(1) * 2 + xh), (h, zp(-1) * 2 + xh), (h, z * 2 + xo)
    z_dev = (dn_dev, up_dev)
    sib_dev = (q * 2 + 1 - core, w)
    chip = lambda j: (q + j + 8) % 8
    peer = lambda j: (chip(j) * 2 + core, w)

    def remote(src, dst, ss, rs, dev):
        return pltpu.make_async_remote_copy(
            src_ref=src, dst_ref=dst, send_sem=ss, recv_sem=rs, device_id=dev, device_id_type=MESH
        )

    loads = [
        pltpu.make_async_copy(tok_in, panel.at[0, q, core], lsem.at[0]),
        pltpu.make_async_copy(og_in, panel.at[1, q, core], lsem.at[1]),
        pltpu.make_async_copy(gw_in, gw, lsem.at[2]),
        pltpu.make_async_copy(uw_in, uw, lsem.at[3]),
        pltpu.make_async_copy(dw_in, dw, lsem.at[4]),
        pltpu.make_async_copy(cap_hbm, cap_in, lsem.at[5]),
    ]
    for c in loads:
        c.start()

    bar = pltpu.get_barrier_semaphore()
    for dev in (up_dev, dn_dev, x_dev, sib_dev):
        pl.semaphore_signal(bar, inc=1, device_id=dev, device_id_type=MESH)
    for j in range(1, 8):
        pl.semaphore_signal(bar, inc=1, device_id=peer(j), device_id_type=MESH)
    pl.semaphore_wait(bar, 11)

    def tok_copy(p, j):
        mine = panel.at[p, q, core]
        return remote(mine, mine, tok_ss, tok_rs.at[p, j], peer(j))

    def fwd_copy(p, j):
        blk = panel.at[p, chip(-j), core]
        return remote(blk, blk, fwd_ss, fwd_rs.at[p], sib_dev)

    def fwd_got(p, j):
        blk = panel.at[p, chip(-j), 1 - core]
        return remote(blk, blk, fwd_ss, fwd_rs.at[p], sib_dev)

    def send(p):
        loads[p].wait()

        @pl.loop(1, 8)
        def _(j):
            tok_copy(p, j).start()

        fwd_copy(p, 0).start()

    def forward(p, lo=1, hi=8):
        @pl.loop(lo, hi)
        def _(j):
            tok_copy(p, j).wait_recv()
            fwd_copy(p, j).start()

    def gathered(p):
        half = panel.at[p, pl.ds(0, 4)]
        remote(half, half, fwd_ss, fwd_rs.at[p], sib_dev).wait_recv()

    def partial(m, rows, col):
        if m == 2:
            return dot(rows, dw[pl.ds(col, TILE), :], 1, 1)
        return dot(rows, (gw, uw)[m][:, pl.ds(col, TILE)], 1, 0)

    def tile(i):
        return pl.ds(i * TILE, TILE)

    def part_a(ms, dst, x, f):
        for m in ms:
            rows = panel[m // 2, :, x].reshape(NZ * NB, 512)
            for i in range(na):
                dst[:, m, :, tile(i)] = f(partial(m, rows, i * TILE)).reshape(NZ, NB, TILE)

    def part_b(ms):
        for m in ms:
            rows = panel[m // 2].reshape(2 * NZ * NB, 512)
            for i in range(nb):
                v = partial(m, rows, wa + i * TILE).reshape(NZ, 2, NB, TILE)
                for x in range(2):
                    pb[:, 3 * x + m, :, tile(i)] = v[:, x]

    def xa_copy(k, g):
        d = zp(k)
        ms = (pl.ds(0, 2), pl.ds(2, 1))[g]
        return remote(xa_s.at[d, ms], xa_r.at[d, ms], xa_ss, xa_rs.at[d], x_dev)

    def hop(dst, own, recv, lo, hi, m0=0, m1=3):
        width = own.shape[-1] // 2

        @pl.loop(m0, m1)
        def _(m):
            for i in range(lo, hi):
                c = pl.ds(i * width, width)
                v = own[m, :, c]
                for r in recv:
                    v = v + dec(r[m, :, c])
                dst[m, :, c] = enc(v) if dst.dtype == BF16 else v

    class Ring:
        def __init__(self, own, s, r, ss, rs):
            self.own, self.s, self.r, self.ss, self.rs = own, s, r, ss, rs
            self.half = s.shape[-1] // 2

        def copy(self, step, d):
            return self.copies(step, d, 0, 3, step - 1)

        def copies(self, step, d, m0, m1, sem):
            ms = pl.ds(m0, m1 - m0)
            src, dst = self.s.at[d, step - 1, ms], self.r.at[d, step - 1, ms]
            if step == 1:
                c = pl.ds(d * self.half, self.half)
                src, dst = src.at[:, :, c], dst.at[:, :, c]
            return remote(src, dst, self.ss.at[min(step - 1, 1)], self.rs.at[d, sem], z_dev[d])

        def first(self, m0, m1, sem):
            for d in range(2):
                own = self.own(zp(4 * (-1, 1)[d]))
                hop(self.s.at[d, 0], own, (), d, d + 1, m0, m1)
                self.copies(1, d, m0, m1, sem).start()

        def second(self, m0, m1, sem):
            for d in range(2):
                own, src, got = self.own(zp(3 * (-1, 1)[d])), self.s.at[d, 1], self.r.at[d, 0]
                self.copies(1, d, m0, m1, sem).wait_recv()
                hop(src, own, (got,), d, d + 1, m0, m1)
                hop(src, own, (), 1 - d, 2 - d, m0, m1)
                self.copies(2, d, m0, m1, sem + 1).start()

        def step(self, step, split=False):
            for d in range(2):
                own = self.own(zp((5 - step) * (-1, 1)[d]))
                src = self.s.at[d, step - 1]
                if step == 1:
                    hop(src, own, (), d, d + 1)
                else:
                    if split:
                        self.copies(step - 1, d, 0, 2, step - 2).wait_recv()
                        self.copies(step - 1, d, 2, 3, step + 2).wait_recv()
                    else:
                        self.copy(step - 1, d).wait_recv()
                    got = self.r.at[d, step - 2]
                    if step == 2:
                        hop(src, own, (got,), d, d + 1)
                        hop(src, own, (), 1 - d, 2 - d)
                    else:
                        hop(src, own, (got,), 0, 2)
                self.copy(step, d).start()

        def finish(self, dst):
            for d in range(2):
                self.copy(4, d).wait_recv()
            hop(dst, self.own(z), (self.r.at[0, 3], self.r.at[1, 3]), 0, 2)

        def drain(self):
            one, rest = self.s.at[0, 0], self.s.at[:, pl.ds(1, 3)]
            remote(one, one, self.ss.at[0], self.rs.at[0, 0], z_dev[0]).wait_send()
            remote(rest, rest, self.ss.at[1], self.rs.at[0, 0], z_dev[0]).wait_send()

    ha = wa // 2
    cols_a = (pl.ds(0, ha), pl.ds(ha, ha))
    xs = (xo, xh)
    rings_a = [
        Ring(lambda d, c=cols_a[i]: pa.at[d, :, :, c], sa.at[i], ra.at[i], za_ss.at[i], za_rs.at[i]) for i in range(2)
    ]
    rings_b = [
        Ring(lambda d, x=xs[i]: pb.at[d, pl.ds(3 * x, 3)], sb.at[i], rb.at[i], zb_ss.at[i], zb_rs.at[i])
        for i in range(2)
    ]

    def step_a(step):
        for ring in rings_a:
            ring.step(step)

    def step_b(step):
        for ring in rings_b:
            ring.step(step, split=step == 3)

    order = (4, 3, -3, 2, -2, 1, -1, 0)
    send(0)
    send(1)
    forward(0)
    gathered(0)
    loads[2].wait()
    loads[3].wait()
    part_a((0, 1), xa_s, xo, enc)
    for k in order[:2]:
        xa_copy(k, 0).start()
    forward(1, 1, 5)
    part_b((0, 1))
    for ring in rings_b:
        ring.first(0, 2, 0)
    forward(1, 5)
    gathered(1)
    loads[4].wait()
    loads[5].wait()
    part_b((2,))
    for ring in rings_b:
        ring.first(2, 3, 4)
    part_a((2,), xa_s, xo, enc)
    for k in order[:2]:
        xa_copy(k, 1).start()
    for k in order[2:]:
        for g in range(2):
            xa_copy(k, g).start()
    for ring in rings_b:
        ring.second(0, 2, 0)
    part_a((0, 1, 2), pa, xh, lambda v: v)

    def take_x(k):
        d = zp(k)
        remote(xa_s.at[d], xa_r.at[d], xa_ss, xa_rs.at[d], x_dev).wait_recv()
        hop(pa.at[d], pa.at[d], (xa_r.at[d],), 0, 2)

    for ring in rings_b:
        ring.second(2, 3, 4)
    take_x(4)
    step_a(1)
    for s, ks in ((2, (3, -3)), (3, (2, -2))):
        step_b(s + 1)
        for k in ks:
            take_x(k)
        step_a(s)
    rings_b[0].finish(xb_s)
    xb_copy = remote(xb_s, xb_r, xb_ss, xb_rs, x_dev)
    xb_copy.start()
    for k in (1, -1):
        take_x(k)
    step_a(4)
    take_x(0)
    own_b = pb.at[z, pl.ds(3 * xh, 3)]
    rings_b[1].finish(own_b)

    def local(src, dst, n, base):
        for i in range(n):
            gate, up, cap_grad = src[0, :, tile(i)], src[1, :, tile(i)], src[2, :, tile(i)]
            at = 2 * (base + i)
            codes = jnp.concatenate([cap_in[at : at + 1, :], cap_in[at + 1 : at + 2, :]], axis=1)
            cap = codes.astype(F32) * (1.0 / 512.0)
            sig = 1.0 / (1.0 + jnp.exp(-gate))
            act = gate * sig
            squash = jnp.tanh(act * up / cap)
            hid_grad = cap_grad * (1.0 - squash * squash)
            dst[0, :, tile(i)] = (cap * squash).astype(BF16)
            dst[1, :, tile(i)] = (hid_grad * up * sig * (1.0 + gate * (1.0 - sig))).astype(BF16)
            dst[2, :, tile(i)] = (hid_grad * act).astype(BF16)

    def halves(blk, step, d, width):
        return blk.at[:, :, pl.ds(d * (width // 2), width // 2)] if step == 4 else blk

    def gza_copy(i, step, d, got=False):
        blk = ga.at[zp((step if got else step - 1) * (1, -1)[d]), xh, :, :, cols_a[i]]
        blk = halves(blk, step, d, ha)
        return remote(blk, blk, gza_ss.at[step // 4], gza_rs.at[i, d, step - 1], z_dev[d])

    def phase(k):
        return 0 if abs(k) < 3 else 1 if abs(k) == 3 else 2

    def gxa_copy(i, k):
        blk = ga.at[zp(k), xh, :, :, cols_a[i]]
        return remote(blk, blk, gxa_ss, gxa_rs.at[phase(k)], x_dev)

    def gzb_copy(i, step, d, got=False):
        blk = gb.at[zp((step if got else step - 1) * (1, -1)[d]), pl.ds(3 * xs[i], 3)]
        blk = halves(blk, step, d, wb)
        return remote(blk, blk, gzb_ss.at[step // 4], gzb_rs.at[i, d, step - 1], z_dev[d])

    xb_copy.wait()
    hop(own_b, own_b, (xb_r,), 0, 2)
    local(own_b, gb.at[z, pl.ds(3 * xh, 3)], nb, na)

    def gxb_copy(x):
        blk = gb.at[z, pl.ds(3 * x, 3)]
        return remote(blk, blk, gxb_ss, gxb_rs, x_dev)

    gxb_copy(xh).start()
    for d in range(2):
        gzb_copy(1, 1, d).start()
    for i in range(2):
        own_a = pa.at[z, :, :, cols_a[i]]
        rings_a[i].finish(own_a)
        local(own_a, ga.at[z, xh, :, :, cols_a[i]], na // 2, i * (na // 2))
        for d in range(2):
            gza_copy(i, 1, d).start()
        gxa_copy(i, 0).start()

    def keep_a(k, x):
        d = zp(k)
        t = pl.multiple_of((d * 2 + x) * NB, NB)
        return pltpu.make_async_copy(ga.at[d, x], d_out.at[:, pl.ds(t, NB), pl.ds(0, wa)], dsem.at[0])

    def keep_b(k, x):
        d = zp(k)
        t = pl.multiple_of((d * 2 + x) * NB, NB)
        return pltpu.make_async_copy(
            gb.at[d, pl.ds(3 * x, 3)], d_out.at[:, pl.ds(t, NB), pl.ds(wa, wb)], dsem.at[1]
        )

    def keep_bs(k):
        for x in range(2):
            keep_b(k, x).start()

    keep_a(0, xh).start()
    keep_panel = pltpu.make_async_copy(panel, panel_out, lsem.at[0])
    keep_panel.start()

    def ig_rows(ks, a=True, b=True):
        def rows(ref):
            return jnp.concatenate([ref(zp(k), x) for k in ks for x in range(2)], axis=0)

        v = 0.0
        for m, wt in ((1, gw), (2, uw)):
            if a:
                v = v + dot(rows(lambda d, x: ga[d, x, m]), wt[:, :wa], 1, 1)
            if b:
                v = v + dot(rows(lambda d, x: gb[d, 3 * x + m]), wt[:, wa:], 1, 1)
        for n_k, k in enumerate(ks):
            part = v[n_k * 2 * NB : (n_k + 1) * 2 * NB].reshape(2, NB, 512)
            ig_acc[zp(k)] = part if b else ig_acc[zp(k)] + part
        if not a:
            return
        for k in ks:
            d = zp(k)
            sib_s[d] = ig_acc[d, 1 - core].astype(BF16)
            sib_copy(k).start()

    def ig_send(ks, n):
        blocks = sib_s.at[pl.ds(0, len(ks))]
        remote(blocks, blocks, sib_ss, sib_rs.at[n], sib_dev).wait_recv()
        for k in ks:
            d = zp(k)
            ig_s[d] = (ig_acc[d, core] + sib_r[d].astype(F32)).astype(BF16)

            @pl.when(d != q)
            def _():
                ig_copy((d - q + 8) % 8).start()

    def ig_copy(j):
        return remote(ig_s.at[chip(j)], ig_out.at[j], ig_ss, ig_rs, peer(j))

    def sib_copy(k):
        d = zp(k)
        return remote(sib_s.at[d], sib_r.at[d], sib_ss, sib_rs.at[phase(k)], sib_dev)

    def take_gx(ks, n):
        blocks = xa_s.at[pl.ds(0, len(ks))]
        remote(blocks, blocks, gxa_ss, gxa_rs.at[n], x_dev).wait_recv()
        for k in ks:
            keep_a(k, xo).start()

    def forward_a(step):
        for i in range(2):
            for d in range(2):
                k = (step - 1) * (1, -1)[d]
                gza_copy(i, step - 1, d, True).wait_recv()
                gza_copy(i, step, d).start()
                gxa_copy(i, k).start()
                if i == 1:
                    keep_a(k, xh).start()

    def forward_b(i, step):
        for d in range(2):
            gzb_copy(i, step - 1, d, True).wait_recv()
            gzb_copy(i, step, d).start()
            keep_b((step - 1) * (1, -1)[d], xs[i]).start()

    forward_a(2)
    gxb_copy(xo).wait_recv()
    for d in range(2):
        gzb_copy(0, 1, d).start()
    keep_bs(0)
    forward_b(1, 2)
    forward_a(3)
    forward_b(0, 2)
    forward_a(4)
    forward_b(1, 3)
    forward_b(0, 3)

    def sent(ref, sem):
        remote(ref, ref, sem, gxb_rs, x_dev).wait_send()

    sent(panel.at[0, pl.ds(0, 7)], tok_ss)
    sent(panel.at[0], fwd_ss)
    sent(xa_s, xa_ss)
    for ring in rings_a + rings_b:
        ring.drain()
    early = (0, 1, -1, 2, -2)
    take_gx(early, 0)
    ig_rows(early)
    for i in range(2):
        for d in range(2):
            gza_copy(i, 4, d, True).wait_recv()
        gxa_copy(i, 4).start()
    keep_a(4, xh).start()
    forward_b(1, 4)
    forward_b(0, 4)
    ig_send(early, 0)
    take_gx((3, -3), 1)
    ig_rows((3, -3))
    ig_send((3, -3), 1)
    for i in (1, 0):
        for d in range(2):
            gzb_copy(i, 4, d, True).wait_recv()
    keep_bs(4)
    ig_rows((4,), a=False)
    take_gx((4,), 2)
    ig_rows((4,), b=False)
    ig_send((4,), 2)
    last = pltpu.make_async_copy(ig_s.at[q], ig_out.at[0], lsem.at[1])
    last.start()

    sent(xa_s, gxa_ss)
    sent(sib_s, sib_ss)
    sent(sa.at[:, 0, 0], gza_ss.at[1])
    sent(sa.at[:, :, pl.ds(0, 3)], gza_ss.at[0])
    sent(sb.at[:, 0, 0], gzb_ss.at[1])
    sent(sb.at[:, :, pl.ds(0, 3)], gzb_ss.at[0])
    gxb_copy(xh).wait_send()

    pieces = pl.ds(0, 7)
    remote(ig_s.at[pieces], ig_out.at[pl.ds(1, 7)], ig_ss, ig_rs, x_dev).wait()
    pltpu.make_async_copy(ga, ga, dsem.at[0]).wait()
    pltpu.make_async_copy(gb, gb, dsem.at[1]).wait()
    keep_panel.wait()
    last.wait()


def weight_grads(
    d_in, panel_in, ig_in, ig_out, gg_out, ug_out, dg_out, d, panel, gg, ug, dg, ig_v, ig_b, isem, osem
):
    first, rest = pl.ds(0, 2 * TILE), pl.ds(2 * TILE, d.shape[2] - 2 * TILE)
    loads = []
    for src, dst in (
        (panel_in.at[0], panel.at[0]),
        (d_in.at[1, :, first], d.at[1, :, first]),
        (d_in.at[1, :, rest], d.at[1, :, rest]),
        (d_in.at[2], d.at[2]),
        (panel_in.at[1], panel.at[1]),
        (d_in.at[0], d.at[0]),
        (ig_in, ig_v),
    ):
        loads.append(pltpu.make_async_copy(src, dst, isem.at[len(loads)]))
        loads[-1].start()
    n = d.shape[2] // TILE
    stores = []

    def store(src, dst):
        stores.append(pltpu.make_async_copy(src, dst, osem.at[len(stores)]))
        stores[-1].start()

    loads[0].wait()
    loads[1].wait()
    for m, dst, out in ((1, gg, gg_out), (2, ug, ug_out)):
        for i in range(n):
            if (m, i) == (1, 2):
                loads[2].wait()
            if (m, i) == (2, 0):
                loads[3].wait()
            c = pl.ds(i * TILE, TILE)
            dst[:, c] = dot(panel[0], d[m, :, c], 0, 0).astype(BF16)
        store(dst, out)
    loads[6].wait()
    ig_b[...] = sum(ig_v[j].astype(F32) for j in range(8)).astype(BF16)
    store(ig_b, ig_out)
    loads[4].wait()
    loads[5].wait()
    for lo, hi in ((0, 4), (4, 6), (6, 7)):
        for i in range(lo, hi):
            c = pl.ds(i * TILE, TILE)
            dg[c, :] = dot(d[0, :, c], panel[1], 0, 0).astype(BF16)
        rows = pl.ds(lo * TILE, (hi - lo) * TILE)
        store(dg.at[rows], dg_out.at[rows])
    for c in stores:
        c.wait()


def per_device(tokens, out_grad, gate_weight, up_weight, down_weight, cap_codes):
    hidden = gate_weight.shape[1]
    n = hidden // TILE
    na = 4
    nb = n - na
    wa, wb = na * TILE, nb * TILE
    dma = pltpu.SemaphoreType.DMA
    sh = jax.ShapeDtypeStruct
    scratch = [
        pltpu.VMEM((512, hidden), BF16),
        pltpu.VMEM((512, hidden), BF16),
        pltpu.VMEM((hidden, 512), BF16),
        pltpu.VMEM((2, NZ, 2, NB, 512), BF16),
        pltpu.VMEM((hidden // 128, 128), jnp.int32),
        pltpu.VMEM((NZ, 3, NB, wa), F32),
        pltpu.VMEM((NZ, 6, NB, wb), F32),
        pltpu.VMEM((NZ, 3, NB, wa), BF16),
        pltpu.VMEM((NZ, 3, NB, wa), BF16),
        pltpu.VMEM((2, 2, 4, 3, NB, wa // 2), BF16),
        pltpu.VMEM((2, 2, 4, 3, NB, wa // 2), BF16),
        pltpu.VMEM((2, 2, 4, 3, NB, wb), BF16),
        pltpu.VMEM((2, 2, 4, 3, NB, wb), BF16),
        pltpu.VMEM((3, NB, wb), BF16),
        pltpu.VMEM((3, NB, wb), BF16),
        pltpu.VMEM((NZ, 2, 3, NB, wa), BF16),
        pltpu.VMEM((NZ, 6, NB, wb), BF16),
        pltpu.VMEM((NZ, 2, NB, 512), F32),
        pltpu.VMEM((NZ, NB, 512), BF16),
        pltpu.VMEM((NZ, NB, 512), BF16),
        pltpu.VMEM((NZ, NB, 512), BF16),
        dma((6,)), dma((2,)),
        dma, dma((2, 8)),
        dma, dma((2,)),
        dma, dma((NZ,)),
        dma((2, 2)), dma((2, 2, 4)),
        dma((2, 2)), dma((2, 2, 6)),
        dma, dma,
        dma, dma((3,)),
        dma((2,)), dma((2, 2, 4)),
        dma((2,)), dma((2, 2, 4)),
        dma, dma,
        dma, dma((3,)),
        dma, dma,
    ]
    any_spec = pl.BlockSpec(memory_space=pl.ANY)
    deltas, panel, ig_sum = pl.pallas_call(
        functools.partial(kernel, na, nb),
        out_shape=(sh((3, 512, hidden), BF16), sh((2, NZ, 2, NB, 512), BF16), sh((8, NB, 512), BF16)),
        in_specs=[any_spec] * 6,
        out_specs=[any_spec] * 3,
        scratch_shapes=scratch,
        compiler_params=pltpu.CompilerParams(
            collective_id=0, has_side_effects=True, vmem_limit_bytes=60 << 20
        ),
        name="exchange",
    )(tokens, out_grad, gate_weight, up_weight, down_weight, cap_codes.reshape(hidden // 128, 128))
    return pl.pallas_call(
        weight_grads,
        out_shape=(
            sh((NB, 512), BF16),
            sh((512, hidden), BF16),
            sh((512, hidden), BF16),
            sh((hidden, 512), BF16),
        ),
        in_specs=[any_spec] * 3,
        out_specs=(any_spec,) * 4,
        scratch_shapes=[
            pltpu.VMEM((3, 512, hidden), BF16),
            pltpu.VMEM((2, 512, 512), BF16),
            pltpu.VMEM((512, hidden), BF16),
            pltpu.VMEM((512, hidden), BF16),
            pltpu.VMEM((hidden, 512), BF16),
            pltpu.VMEM((8, NB, 512), BF16),
            pltpu.VMEM((NB, 512), BF16),
            dma((7,)),
            dma((6,)),
        ],
        compiler_params=pltpu.CompilerParams(vmem_limit_bytes=60 << 20),
        name="weight_grads",
    )(deltas, panel.reshape(2, 512, 512), ig_sum)


def solution(mesh):
    return jax.shard_map(
        per_device,
        mesh=mesh,
        in_specs=(
            P("hid", "wid"),
            P("hid", "wid"),
            P("wid", "hid"),
            P("wid", "hid"),
            P("hid", "wid"),
            P("hid"),
        ),
        out_specs=(P("hid", "wid"), P("wid", "hid"), P("wid", "hid"), P("hid", "wid")),
        check_vma=False,
    )
```

```python
import functools

import jax
import jax.numpy as jnp
from jax import lax
from jax.experimental import pallas as pl
from jax.experimental.pallas import tpu as pltpu
from jax.sharding import PartitionSpec as P

MESH = pl.DeviceIdType.MESH
BF16 = jnp.bfloat16
F32 = jnp.float32

TILE = 256
NB = 32
NZ = 8
SCALE = 2.0**18


def dot(a, b, ca, cb):
    return lax.dot_general(a, b, (((ca,), (cb,)), ((), ())), preferred_element_type=F32)


def enc(v):
    u = v * SCALE
    return ((u * jnp.abs(u)) * (u * u)).astype(BF16)


def dec(y):
    y = y.astype(F32)
    root = lax.rsqrt(lax.rsqrt(jnp.maximum(jnp.abs(y), 2e-38)))
    return root * jnp.where(y < 0.0, -1.0 / SCALE, 1.0 / SCALE)


def kernel(
    na, nb,
    tok_in, og_in, gw_in, uw_in, dw_in, cap_hbm,
    d_out, panel_out, ig_out,
    gw, uw, dw, panel, cap_in,
    pa, pb, xa_s, xa_r, sa, ra, sb, rb, xb_s, xb_r,
    ga, gb, ig_acc, sib_s, sib_r, ig_s,
    lsem, dsem, tok_ss, tok_rs, fwd_ss, fwd_rs, xa_ss, xa_rs, za_ss, za_rs, zb_ss, zb_rs, xb_ss, xb_rs,
    gxa_ss, gxa_rs, gza_ss, gza_rs, gzb_ss, gzb_rs, gxb_ss, gxb_rs, sib_ss, sib_rs, ig_ss, ig_rs,
):
    wa, wb = na * TILE, nb * TILE
    h, w = lax.axis_index("hid"), lax.axis_index("wid")
    z, xh = w // 2, w % 2
    xo = 1 - xh
    q, core = h // 2, h % 2
    zp = lambda k: (z + k + NZ) % NZ
    up_dev, dn_dev, x_dev = (h, zp(1) * 2 + xh), (h, zp(-1) * 2 + xh), (h, z * 2 + xo)
    z_dev = (dn_dev, up_dev)
    sib_dev = (q * 2 + 1 - core, w)
    chip = lambda j: (q + j + 8) % 8
    peer = lambda j: (chip(j) * 2 + core, w)

    def remote(src, dst, ss, rs, dev):
        return pltpu.make_async_remote_copy(
            src_ref=src, dst_ref=dst, send_sem=ss, recv_sem=rs, device_id=dev, device_id_type=MESH
        )

    loads = [
        pltpu.make_async_copy(tok_in, panel.at[0, q, core], lsem.at[0]),
        pltpu.make_async_copy(og_in, panel.at[1, q, core], lsem.at[1]),
        pltpu.make_async_copy(gw_in, gw, lsem.at[2]),
        pltpu.make_async_copy(uw_in, uw, lsem.at[3]),
        pltpu.make_async_copy(dw_in, dw, lsem.at[4]),
        pltpu.make_async_copy(cap_hbm, cap_in, lsem.at[5]),
    ]
    for c in loads:
        c.start()

    bar = pltpu.get_barrier_semaphore()
    for dev in (up_dev, dn_dev, x_dev, sib_dev):
        pl.semaphore_signal(bar, inc=1, device_id=dev, device_id_type=MESH)
    for j in range(1, 8):
        pl.semaphore_signal(bar, inc=1, device_id=peer(j), device_id_type=MESH)
    pl.semaphore_wait(bar, 11)

    def tok_copy(p, j):
        mine = panel.at[p, q, core]
        return remote(mine, mine, tok_ss, tok_rs.at[p, j], peer(j))

    def fwd_copy(p, j):
        blk = panel.at[p, chip(-j), core]
        return remote(blk, blk, fwd_ss, fwd_rs.at[p], sib_dev)

    def fwd_got(p, j):
        blk = panel.at[p, chip(-j), 1 - core]
        return remote(blk, blk, fwd_ss, fwd_rs.at[p], sib_dev)

    def send(p):
        loads[p].wait()

        @pl.loop(1, 8)
        def _(j):
            tok_copy(p, j).start()

        fwd_copy(p, 0).start()

    def forward(p, lo=1, hi=8):
        @pl.loop(lo, hi)
        def _(j):
            tok_copy(p, j).wait_recv()
            fwd_copy(p, j).start()

    def gathered(p):
        half = panel.at[p, pl.ds(0, 4)]
        remote(half, half, fwd_ss, fwd_rs.at[p], sib_dev).wait_recv()

    def partial(m, rows, col):
        if m == 2:
            return dot(rows, dw[pl.ds(col, TILE), :], 1, 1)
        return dot(rows, (gw, uw)[m][:, pl.ds(col, TILE)], 1, 0)

    def tile(i):
        return pl.ds(i * TILE, TILE)

    def part_a(ms, dst, x, f):
        for m in ms:
            rows = panel[m // 2, :, x].reshape(NZ * NB, 512)
            for i in range(na):
                dst[:, m, :, tile(i)] = f(partial(m, rows, i * TILE)).reshape(NZ, NB, TILE)

    def part_b(ms):
        for m in ms:
            rows = panel[m // 2].reshape(2 * NZ * NB, 512)
            for i in range(nb):
                v = partial(m, rows, wa + i * TILE).reshape(NZ, 2, NB, TILE)
                for x in range(2):
                    pb[:, 3 * x + m, :, tile(i)] = v[:, x]

    def xa_copy(k, g):
        d = zp(k)
        ms = (pl.ds(0, 2), pl.ds(2, 1))[g]
        return remote(xa_s.at[d, ms], xa_r.at[d, ms], xa_ss, xa_rs.at[d], x_dev)

    def hop(dst, own, recv, lo, hi, m0=0, m1=3):
        width = own.shape[-1] // 2

        @pl.loop(m0, m1)
        def _(m):
            for i in range(lo, hi):
                c = pl.ds(i * width, width)
                v = own[m, :, c]
                for r in recv:
                    v = v + dec(r[m, :, c])
                dst[m, :, c] = enc(v) if dst.dtype == BF16 else v

    class Ring:
        def __init__(self, own, s, r, ss, rs):
            self.own, self.s, self.r, self.ss, self.rs = own, s, r, ss, rs
            self.half = s.shape[-1] // 2

        def copy(self, step, d):
            return self.copies(step, d, 0, 3, step - 1)

        def copies(self, step, d, m0, m1, sem):
            ms = pl.ds(m0, m1 - m0)
            src, dst = self.s.at[d, step - 1, ms], self.r.at[d, step - 1, ms]
            if step == 1:
                c = pl.ds(d * self.half, self.half)
                src, dst = src.at[:, :, c], dst.at[:, :, c]
            return remote(src, dst, self.ss.at[min(step - 1, 1)], self.rs.at[d, sem], z_dev[d])

        def first(self, m0, m1, sem):
            for d in range(2):
                own = self.own(zp(4 * (-1, 1)[d]))
                hop(self.s.at[d, 0], own, (), d, d + 1, m0, m1)
                self.copies(1, d, m0, m1, sem).start()

        def second(self, m0, m1, sem):
            for d in range(2):
                own, src, got = self.own(zp(3 * (-1, 1)[d])), self.s.at[d, 1], self.r.at[d, 0]
                self.copies(1, d, m0, m1, sem).wait_recv()
                hop(src, own, (got,), d, d + 1, m0, m1)
                hop(src, own, (), 1 - d, 2 - d, m0, m1)
                self.copies(2, d, m0, m1, sem + 1).start()

        def step(self, step, split=False):
            for d in range(2):
                own = self.own(zp((5 - step) * (-1, 1)[d]))
                src = self.s.at[d, step - 1]
                if step == 1:
                    hop(src, own, (), d, d + 1)
                else:
                    if split:
                        self.copies(step - 1, d, 0, 2, step - 2).wait_recv()
                        self.copies(step - 1, d, 2, 3, step + 2).wait_recv()
                    else:
                        self.copy(step - 1, d).wait_recv()
                    got = self.r.at[d, step - 2]
                    if step == 2:
                        hop(src, own, (got,), d, d + 1)
                        hop(src, own, (), 1 - d, 2 - d)
                    else:
                        hop(src, own, (got,), 0, 2)
                self.copy(step, d).start()

        def finish(self, dst):
            for d in range(2):
                self.copy(4, d).wait_recv()
            hop(dst, self.own(z), (self.r.at[0, 3], self.r.at[1, 3]), 0, 2)

        def drain(self):
            one, rest = self.s.at[0, 0], self.s.at[:, pl.ds(1, 3)]
            remote(one, one, self.ss.at[0], self.rs.at[0, 0], z_dev[0]).wait_send()
            remote(rest, rest, self.ss.at[1], self.rs.at[0, 0], z_dev[0]).wait_send()

    ha = wa // 2
    cols_a = (pl.ds(0, ha), pl.ds(ha, ha))
    xs = (xo, xh)
    rings_a = [
        Ring(lambda d, c=cols_a[i]: pa.at[d, :, :, c], sa.at[i], ra.at[i], za_ss.at[i], za_rs.at[i]) for i in range(2)
    ]
    rings_b = [
        Ring(lambda d, x=xs[i]: pb.at[d, pl.ds(3 * x, 3)], sb.at[i], rb.at[i], zb_ss.at[i], zb_rs.at[i])
        for i in range(2)
    ]

    def step_a(step):
        for ring in rings_a:
            ring.step(step)

    def step_b(step):
        for ring in rings_b:
            ring.step(step, split=step == 3)

    order = (4, 3, -3, 2, -2, 1, -1, 0)
    send(0)
    forward(0, 1, 2)
    send(1)
    forward(0, 2)
    gathered(0)
    loads[2].wait()
    loads[3].wait()
    part_a((0, 1), xa_s, xo, enc)
    for k in order[:2]:
        xa_copy(k, 0).start()
    forward(1, 1, 5)
    part_b((0, 1))
    for ring in rings_b:
        ring.first(0, 2, 0)
    forward(1, 5)
    gathered(1)
    loads[4].wait()
    loads[5].wait()
    part_b((2,))
    for ring in rings_b:
        ring.first(2, 3, 4)
    part_a((2,), xa_s, xo, enc)
    for k in order[:2]:
        xa_copy(k, 1).start()
    for k in order[2:]:
        for g in range(2):
            xa_copy(k, g).start()
    for ring in rings_b:
        ring.second(0, 2, 0)
    part_a((0, 1, 2), pa, xh, lambda v: v)

    def take_x(k):
        d = zp(k)
        remote(xa_s.at[d], xa_r.at[d], xa_ss, xa_rs.at[d], x_dev).wait_recv()
        hop(pa.at[d], pa.at[d], (xa_r.at[d],), 0, 2)

    for ring in rings_b:
        ring.second(2, 3, 4)
    take_x(4)
    step_a(1)
    for s, ks in ((2, (3, -3)), (3, (2, -2))):
        step_b(s + 1)
        for k in ks:
            take_x(k)
        step_a(s)
    rings_b[0].finish(xb_s)
    xb_copy = remote(xb_s, xb_r, xb_ss, xb_rs, x_dev)
    xb_copy.start()
    for k in (1, -1):
        take_x(k)
    step_a(4)
    take_x(0)
    own_b = pb.at[z, pl.ds(3 * xh, 3)]
    rings_b[1].finish(own_b)

    def local(src, dst, n, base):
        for i in range(n):
            gate, up, cap_grad = src[0, :, tile(i)], src[1, :, tile(i)], src[2, :, tile(i)]
            at = 2 * (base + i)
            codes = jnp.concatenate([cap_in[at : at + 1, :], cap_in[at + 1 : at + 2, :]], axis=1)
            cap = codes.astype(F32) * (1.0 / 512.0)
            sig = 1.0 / (1.0 + jnp.exp(-gate))
            act = gate * sig
            squash = jnp.tanh(act * up / cap)
            hid_grad = cap_grad * (1.0 - squash * squash)
            dst[0, :, tile(i)] = (cap * squash).astype(BF16)
            dst[1, :, tile(i)] = (hid_grad * up * sig * (1.0 + gate * (1.0 - sig))).astype(BF16)
            dst[2, :, tile(i)] = (hid_grad * act).astype(BF16)

    def halves(blk, step, d, width):
        return blk.at[:, :, pl.ds(d * (width // 2), width // 2)] if step == 4 else blk

    def gza_copy(i, step, d, got=False):
        blk = ga.at[zp((step if got else step - 1) * (1, -1)[d]), xh, :, :, cols_a[i]]
        blk = halves(blk, step, d, ha)
        return remote(blk, blk, gza_ss.at[step // 4], gza_rs.at[i, d, step - 1], z_dev[d])

    def phase(k):
        return 0 if abs(k) < 3 else 1 if abs(k) == 3 else 2

    def gxa_copy(i, k):
        blk = ga.at[zp(k), xh, :, :, cols_a[i]]
        return remote(blk, blk, gxa_ss, gxa_rs.at[phase(k)], x_dev)

    def gzb_copy(i, step, d, got=False):
        blk = gb.at[zp((step if got else step - 1) * (1, -1)[d]), pl.ds(3 * xs[i], 3)]
        blk = halves(blk, step, d, wb)
        return remote(blk, blk, gzb_ss.at[step // 4], gzb_rs.at[i, d, step - 1], z_dev[d])

    xb_copy.wait()
    hop(own_b, own_b, (xb_r,), 0, 2)
    local(own_b, gb.at[z, pl.ds(3 * xh, 3)], nb, na)

    def gxb_copy(x):
        blk = gb.at[z, pl.ds(3 * x, 3)]
        return remote(blk, blk, gxb_ss, gxb_rs, x_dev)

    gxb_copy(xh).start()
    for d in range(2):
        gzb_copy(1, 1, d).start()
    for i in range(2):
        own_a = pa.at[z, :, :, cols_a[i]]
        rings_a[i].finish(own_a)
        local(own_a, ga.at[z, xh, :, :, cols_a[i]], na // 2, i * (na // 2))
        for d in range(2):
            gza_copy(i, 1, d).start()
        gxa_copy(i, 0).start()

    def keep_a(k, x):
        d = zp(k)
        t = pl.multiple_of((d * 2 + x) * NB, NB)
        return pltpu.make_async_copy(ga.at[d, x], d_out.at[:, pl.ds(t, NB), pl.ds(0, wa)], dsem.at[0])

    def keep_b(k, x):
        d = zp(k)
        t = pl.multiple_of((d * 2 + x) * NB, NB)
        return pltpu.make_async_copy(
            gb.at[d, pl.ds(3 * x, 3)], d_out.at[:, pl.ds(t, NB), pl.ds(wa, wb)], dsem.at[1]
        )

    def keep_bs(k):
        for x in range(2):
            keep_b(k, x).start()

    keep_a(0, xh).start()
    keep_panel = pltpu.make_async_copy(panel, panel_out, lsem.at[0])
    keep_panel.start()

    def ig_rows(ks, a=True, b=True):
        def rows(ref):
            return jnp.concatenate([ref(zp(k), x) for k in ks for x in range(2)], axis=0)

        v = 0.0
        for m, wt in ((1, gw), (2, uw)):
            if a:
                v = v + dot(rows(lambda d, x: ga[d, x, m]), wt[:, :wa], 1, 1)
            if b:
                v = v + dot(rows(lambda d, x: gb[d, 3 * x + m]), wt[:, wa:], 1, 1)
        for n_k, k in enumerate(ks):
            part = v[n_k * 2 * NB : (n_k + 1) * 2 * NB].reshape(2, NB, 512)
            ig_acc[zp(k)] = part if b else ig_acc[zp(k)] + part
        if not a:
            return
        for k in ks:
            d = zp(k)
            sib_s[d] = ig_acc[d, 1 - core].astype(BF16)
            sib_copy(k).start()

    def ig_send(ks, n):
        blocks = sib_s.at[pl.ds(0, len(ks))]
        remote(blocks, blocks, sib_ss, sib_rs.at[n], sib_dev).wait_recv()
        for k in ks:
            d = zp(k)
            ig_s[d] = (ig_acc[d, core] + sib_r[d].astype(F32)).astype(BF16)

            @pl.when(d != q)
            def _():
                ig_copy((d - q + 8) % 8).start()

    def ig_copy(j):
        return remote(ig_s.at[chip(j)], ig_out.at[j], ig_ss, ig_rs, peer(j))

    def sib_copy(k):
        d = zp(k)
        return remote(sib_s.at[d], sib_r.at[d], sib_ss, sib_rs.at[phase(k)], sib_dev)

    def take_gx(ks, n):
        blocks = xa_s.at[pl.ds(0, len(ks))]
        remote(blocks, blocks, gxa_ss, gxa_rs.at[n], x_dev).wait_recv()
        for k in ks:
            keep_a(k, xo).start()

    def forward_a(step):
        for i in range(2):
            for d in range(2):
                k = (step - 1) * (1, -1)[d]
                gza_copy(i, step - 1, d, True).wait_recv()
                gza_copy(i, step, d).start()
                gxa_copy(i, k).start()
                if i == 1:
                    keep_a(k, xh).start()

    def forward_b(i, step):
        for d in range(2):
            gzb_copy(i, step - 1, d, True).wait_recv()
            gzb_copy(i, step, d).start()
            keep_b((step - 1) * (1, -1)[d], xs[i]).start()

    forward_a(2)
    gxb_copy(xo).wait_recv()
    for d in range(2):
        gzb_copy(0, 1, d).start()
    keep_bs(0)
    forward_b(1, 2)
    forward_a(3)
    forward_b(0, 2)
    forward_b(1, 3)
    forward_a(4)
    forward_b(0, 3)

    def sent(ref, sem):
        remote(ref, ref, sem, gxb_rs, x_dev).wait_send()

    sent(panel.at[0, pl.ds(0, 7)], tok_ss)
    sent(panel.at[0], fwd_ss)
    sent(xa_s, xa_ss)
    for ring in rings_a + rings_b:
        ring.drain()
    early = (0, 1, -1, 2, -2)
    take_gx(early, 0)
    ig_rows(early)
    for i in range(2):
        for d in range(2):
            gza_copy(i, 4, d, True).wait_recv()
        gxa_copy(i, 4).start()
    keep_a(4, xh).start()
    forward_b(1, 4)
    forward_b(0, 4)
    ig_send(early, 0)
    take_gx((3, -3), 1)
    ig_rows((3, -3))
    ig_send((3, -3), 1)
    for i in (1, 0):
        for d in range(2):
            gzb_copy(i, 4, d, True).wait_recv()
    keep_bs(4)
    ig_rows((4,), a=False)
    take_gx((4,), 2)
    ig_rows((4,), b=False)
    ig_send((4,), 2)
    last = pltpu.make_async_copy(ig_s.at[q], ig_out.at[0], lsem.at[1])
    last.start()

    sent(xa_s, gxa_ss)
    sent(sib_s, sib_ss)
    sent(sa.at[:, 0, 0], gza_ss.at[1])
    sent(sa.at[:, :, pl.ds(0, 3)], gza_ss.at[0])
    sent(sb.at[:, 0, 0], gzb_ss.at[1])
    sent(sb.at[:, :, pl.ds(0, 3)], gzb_ss.at[0])
    gxb_copy(xh).wait_send()

    pieces = pl.ds(0, 7)
    remote(ig_s.at[pieces], ig_out.at[pl.ds(1, 7)], ig_ss, ig_rs, x_dev).wait()
    pltpu.make_async_copy(ga, ga, dsem.at[0]).wait()
    pltpu.make_async_copy(gb, gb, dsem.at[1]).wait()
    keep_panel.wait()
    last.wait()


def weight_grads(
    d_in, panel_in, ig_in, ig_out, gg_out, ug_out, dg_out, d, panel, gg, ug, dg, ig_v, ig_b, isem, osem
):
    first, rest = pl.ds(0, 2 * TILE), pl.ds(2 * TILE, d.shape[2] - 2 * TILE)
    loads = []
    for src, dst in (
        (panel_in.at[0], panel.at[0]),
        (d_in.at[1, :, first], d.at[1, :, first]),
        (d_in.at[1, :, rest], d.at[1, :, rest]),
        (d_in.at[2], d.at[2]),
        (panel_in.at[1], panel.at[1]),
        (d_in.at[0], d.at[0]),
        (ig_in, ig_v),
    ):
        loads.append(pltpu.make_async_copy(src, dst, isem.at[len(loads)]))
        loads[-1].start()
    n = d.shape[2] // TILE
    stores = []

    def store(src, dst):
        stores.append(pltpu.make_async_copy(src, dst, osem.at[len(stores)]))
        stores[-1].start()

    loads[0].wait()
    loads[1].wait()
    for m, dst, out in ((1, gg, gg_out), (2, ug, ug_out)):
        for i in range(n):
            if (m, i) == (1, 2):
                loads[2].wait()
            if (m, i) == (2, 0):
                loads[3].wait()
            c = pl.ds(i * TILE, TILE)
            dst[:, c] = dot(panel[0], d[m, :, c], 0, 0).astype(BF16)
        store(dst, out)
    loads[6].wait()
    ig_b[...] = sum(ig_v[j].astype(F32) for j in range(8)).astype(BF16)
    store(ig_b, ig_out)
    loads[4].wait()
    loads[5].wait()
    for lo, hi in ((0, 4), (4, 6), (6, 7)):
        for i in range(lo, hi):
            c = pl.ds(i * TILE, TILE)
            dg[c, :] = dot(d[0, :, c], panel[1], 0, 0).astype(BF16)
        rows = pl.ds(lo * TILE, (hi - lo) * TILE)
        store(dg.at[rows], dg_out.at[rows])
    for c in stores:
        c.wait()


def per_device(tokens, out_grad, gate_weight, up_weight, down_weight, cap_codes):
    hidden = gate_weight.shape[1]
    n = hidden // TILE
    na = 4
    nb = n - na
    wa, wb = na * TILE, nb * TILE
    dma = pltpu.SemaphoreType.DMA
    sh = jax.ShapeDtypeStruct
    scratch = [
        pltpu.VMEM((512, hidden), BF16),
        pltpu.VMEM((512, hidden), BF16),
        pltpu.VMEM((hidden, 512), BF16),
        pltpu.VMEM((2, NZ, 2, NB, 512), BF16),
        pltpu.VMEM((hidden // 128, 128), jnp.int32),
        pltpu.VMEM((NZ, 3, NB, wa), F32),
        pltpu.VMEM((NZ, 6, NB, wb), F32),
        pltpu.VMEM((NZ, 3, NB, wa), BF16),
        pltpu.VMEM((NZ, 3, NB, wa), BF16),
        pltpu.VMEM((2, 2, 4, 3, NB, wa // 2), BF16),
        pltpu.VMEM((2, 2, 4, 3, NB, wa // 2), BF16),
        pltpu.VMEM((2, 2, 4, 3, NB, wb), BF16),
        pltpu.VMEM((2, 2, 4, 3, NB, wb), BF16),
        pltpu.VMEM((3, NB, wb), BF16),
        pltpu.VMEM((3, NB, wb), BF16),
        pltpu.VMEM((NZ, 2, 3, NB, wa), BF16),
        pltpu.VMEM((NZ, 6, NB, wb), BF16),
        pltpu.VMEM((NZ, 2, NB, 512), F32),
        pltpu.VMEM((NZ, NB, 512), BF16),
        pltpu.VMEM((NZ, NB, 512), BF16),
        pltpu.VMEM((NZ, NB, 512), BF16),
        dma((6,)), dma((2,)),
        dma, dma((2, 8)),
        dma, dma((2,)),
        dma, dma((NZ,)),
        dma((2, 2)), dma((2, 2, 4)),
        dma((2, 2)), dma((2, 2, 6)),
        dma, dma,
        dma, dma((3,)),
        dma((2,)), dma((2, 2, 4)),
        dma((2,)), dma((2, 2, 4)),
        dma, dma,
        dma, dma((3,)),
        dma, dma,
    ]
    any_spec = pl.BlockSpec(memory_space=pl.ANY)
    deltas, panel, ig_sum = pl.pallas_call(
        functools.partial(kernel, na, nb),
        out_shape=(sh((3, 512, hidden), BF16), sh((2, NZ, 2, NB, 512), BF16), sh((8, NB, 512), BF16)),
        in_specs=[any_spec] * 6,
        out_specs=[any_spec] * 3,
        scratch_shapes=scratch,
        compiler_params=pltpu.CompilerParams(
            collective_id=0, has_side_effects=True, vmem_limit_bytes=60 << 20
        ),
        name="exchange",
    )(tokens, out_grad, gate_weight, up_weight, down_weight, cap_codes.reshape(hidden // 128, 128))
    return pl.pallas_call(
        weight_grads,
        out_shape=(
            sh((NB, 512), BF16),
            sh((512, hidden), BF16),
            sh((512, hidden), BF16),
            sh((hidden, 512), BF16),
        ),
        in_specs=[any_spec] * 3,
        out_specs=(any_spec,) * 4,
        scratch_shapes=[
            pltpu.VMEM((3, 512, hidden), BF16),
            pltpu.VMEM((2, 512, 512), BF16),
            pltpu.VMEM((512, hidden), BF16),
            pltpu.VMEM((512, hidden), BF16),
            pltpu.VMEM((hidden, 512), BF16),
            pltpu.VMEM((8, NB, 512), BF16),
            pltpu.VMEM((NB, 512), BF16),
            dma((7,)),
            dma((6,)),
        ],
        compiler_params=pltpu.CompilerParams(vmem_limit_bytes=60 << 20),
        name="weight_grads",
    )(deltas, panel.reshape(2, 512, 512), ig_sum)


def solution(mesh):
    return jax.shard_map(
        per_device,
        mesh=mesh,
        in_specs=(
            P("hid", "wid"),
            P("hid", "wid"),
            P("wid", "hid"),
            P("wid", "hid"),
            P("hid", "wid"),
            P("hid"),
        ),
        out_specs=(P("hid", "wid"), P("wid", "hid"), P("wid", "hid"), P("hid", "wid")),
        check_vma=False,
    )
```

```python
import functools

import jax
import jax.numpy as jnp
from jax import lax
from jax.experimental import pallas as pl
from jax.experimental.pallas import tpu as pltpu
from jax.sharding import PartitionSpec as P

MESH = pl.DeviceIdType.MESH
BF16 = jnp.bfloat16
F32 = jnp.float32

TILE = 256
NB = 32
NZ = 8
SCALE = 2.0**18


def dot(a, b, ca, cb):
    return lax.dot_general(a, b, (((ca,), (cb,)), ((), ())), preferred_element_type=F32)


def enc(v):
    u = v * SCALE
    return ((u * jnp.abs(u)) * (u * u)).astype(BF16)


def dec(y):
    y = y.astype(F32)
    root = lax.rsqrt(lax.rsqrt(jnp.maximum(jnp.abs(y), 2e-38)))
    return root * jnp.where(y < 0.0, -1.0 / SCALE, 1.0 / SCALE)


def kernel(
    na, nb,
    tok_in, og_in, gw_in, uw_in, dw_in, cap_hbm,
    d_out, panel_out, ig_out,
    gw, uw, dw, panel, cap_in,
    pa, pb, xa_s, xa_r, sa, ra, sb, rb, xb_s, xb_r,
    ga, gb, ig_acc, sib_s, sib_r, ig_s,
    lsem, dsem, tok_ss, tok_rs, fwd_ss, fwd_rs, xa_ss, xa_rs, za_ss, za_rs, zb_ss, zb_rs, xb_ss, xb_rs,
    gxa_ss, gxa_rs, gza_ss, gza_rs, gzb_ss, gzb_rs, gxb_ss, gxb_rs, sib_ss, sib_rs, ig_ss, ig_rs,
):
    wa, wb = na * TILE, nb * TILE
    h, w = lax.axis_index("hid"), lax.axis_index("wid")
    z, xh = w // 2, w % 2
    xo = 1 - xh
    q, core = h // 2, h % 2
    zp = lambda k: (z + k + NZ) % NZ
    up_dev, dn_dev, x_dev = (h, zp(1) * 2 + xh), (h, zp(-1) * 2 + xh), (h, z * 2 + xo)
    z_dev = (dn_dev, up_dev)
    sib_dev = (q * 2 + 1 - core, w)
    chip = lambda j: (q + j + 8) % 8
    peer = lambda j: (chip(j) * 2 + core, w)

    def remote(src, dst, ss, rs, dev):
        return pltpu.make_async_remote_copy(
            src_ref=src, dst_ref=dst, send_sem=ss, recv_sem=rs, device_id=dev, device_id_type=MESH
        )

    loads = [
        pltpu.make_async_copy(tok_in, panel.at[0, q, core], lsem.at[0]),
        pltpu.make_async_copy(og_in, panel.at[1, q, core], lsem.at[1]),
        pltpu.make_async_copy(gw_in, gw, lsem.at[2]),
        pltpu.make_async_copy(uw_in, uw, lsem.at[3]),
        pltpu.make_async_copy(dw_in, dw, lsem.at[4]),
        pltpu.make_async_copy(cap_hbm, cap_in, lsem.at[5]),
    ]
    for c in loads:
        c.start()

    bar = pltpu.get_barrier_semaphore()
    for dev in (up_dev, dn_dev, x_dev, sib_dev):
        pl.semaphore_signal(bar, inc=1, device_id=dev, device_id_type=MESH)
    for j in range(1, 8):
        pl.semaphore_signal(bar, inc=1, device_id=peer(j), device_id_type=MESH)
    pl.semaphore_wait(bar, 11)

    def tok_copy(p, j):
        mine = panel.at[p, q, core]
        return remote(mine, mine, tok_ss, tok_rs.at[p, j], peer(j))

    def fwd_copy(p, j):
        blk = panel.at[p, chip(-j), core]
        return remote(blk, blk, fwd_ss, fwd_rs.at[p], sib_dev)

    def fwd_got(p, j):
        blk = panel.at[p, chip(-j), 1 - core]
        return remote(blk, blk, fwd_ss, fwd_rs.at[p], sib_dev)

    def send(p):
        loads[p].wait()

        @pl.loop(1, 8)
        def _(j):
            tok_copy(p, j).start()

        fwd_copy(p, 0).start()

    def forward(p, lo=1, hi=8):
        @pl.loop(lo, hi)
        def _(j):
            tok_copy(p, j).wait_recv()
            fwd_copy(p, j).start()

    def gathered(p):
        half = panel.at[p, pl.ds(0, 4)]
        remote(half, half, fwd_ss, fwd_rs.at[p], sib_dev).wait_recv()

    def partial(m, rows, col):
        if m == 2:
            return dot(rows, dw[pl.ds(col, TILE), :], 1, 1)
        return dot(rows, (gw, uw)[m][:, pl.ds(col, TILE)], 1, 0)

    def tile(i):
        return pl.ds(i * TILE, TILE)

    def part_a(ms, dst, x, f):
        for m in ms:
            rows = panel[m // 2, :, x].reshape(NZ * NB, 512)
            for i in range(na):
                dst[:, m, :, tile(i)] = f(partial(m, rows, i * TILE)).reshape(NZ, NB, TILE)

    def part_b(ms):
        for m in ms:
            rows = panel[m // 2].reshape(2 * NZ * NB, 512)
            for i in range(nb):
                v = partial(m, rows, wa + i * TILE).reshape(NZ, 2, NB, TILE)
                for x in range(2):
                    pb[:, 3 * x + m, :, tile(i)] = v[:, x]

    def xa_copy(k, g):
        d = zp(k)
        ms = (pl.ds(0, 2), pl.ds(2, 1))[g]
        return remote(xa_s.at[d, ms], xa_r.at[d, ms], xa_ss, xa_rs.at[d], x_dev)

    def hop(dst, own, recv, lo, hi, m0=0, m1=3):
        width = own.shape[-1] // 2

        @pl.loop(m0, m1)
        def _(m):
            for i in range(lo, hi):
                c = pl.ds(i * width, width)
                v = own[m, :, c]
                for r in recv:
                    v = v + dec(r[m, :, c])
                dst[m, :, c] = enc(v) if dst.dtype == BF16 else v

    class Ring:
        def __init__(self, own, s, r, ss, rs):
            self.own, self.s, self.r, self.ss, self.rs = own, s, r, ss, rs
            self.half = s.shape[-1] // 2

        def copy(self, step, d):
            return self.copies(step, d, 0, 3, step - 1)

        def copies(self, step, d, m0, m1, sem):
            ms = pl.ds(m0, m1 - m0)
            src, dst = self.s.at[d, step - 1, ms], self.r.at[d, step - 1, ms]
            if step == 1:
                c = pl.ds(d * self.half, self.half)
                src, dst = src.at[:, :, c], dst.at[:, :, c]
            return remote(src, dst, self.ss.at[min(step - 1, 1)], self.rs.at[d, sem], z_dev[d])

        def first(self, m0, m1, sem):
            for d in range(2):
                own = self.own(zp(4 * (-1, 1)[d]))
                hop(self.s.at[d, 0], own, (), d, d + 1, m0, m1)
                self.copies(1, d, m0, m1, sem).start()

        def second(self, m0, m1, sem):
            for d in range(2):
                own, src, got = self.own(zp(3 * (-1, 1)[d])), self.s.at[d, 1], self.r.at[d, 0]
                self.copies(1, d, m0, m1, sem).wait_recv()
                hop(src, own, (got,), d, d + 1, m0, m1)
                hop(src, own, (), 1 - d, 2 - d, m0, m1)
                self.copies(2, d, m0, m1, sem + 1).start()

        def step(self, step, split=False):
            for d in range(2):
                own = self.own(zp((5 - step) * (-1, 1)[d]))
                src = self.s.at[d, step - 1]
                if step == 1:
                    hop(src, own, (), d, d + 1)
                else:
                    if split:
                        self.copies(step - 1, d, 0, 2, step - 2).wait_recv()
                        self.copies(step - 1, d, 2, 3, step + 2).wait_recv()
                    else:
                        self.copy(step - 1, d).wait_recv()
                    got = self.r.at[d, step - 2]
                    if step == 2:
                        hop(src, own, (got,), d, d + 1)
                        hop(src, own, (), 1 - d, 2 - d)
                    else:
                        hop(src, own, (got,), 0, 2)
                self.copy(step, d).start()

        def finish(self, dst):
            for d in range(2):
                self.copy(4, d).wait_recv()
            hop(dst, self.own(z), (self.r.at[0, 3], self.r.at[1, 3]), 0, 2)

        def drain(self):
            one, rest = self.s.at[0, 0], self.s.at[:, pl.ds(1, 3)]
            remote(one, one, self.ss.at[0], self.rs.at[0, 0], z_dev[0]).wait_send()
            remote(rest, rest, self.ss.at[1], self.rs.at[0, 0], z_dev[0]).wait_send()

    ha = wa // 2
    cols_a = (pl.ds(0, ha), pl.ds(ha, ha))
    xs = (xo, xh)
    rings_a = [
        Ring(lambda d, c=cols_a[i]: pa.at[d, :, :, c], sa.at[i], ra.at[i], za_ss.at[i], za_rs.at[i]) for i in range(2)
    ]
    rings_b = [
        Ring(lambda d, x=xs[i]: pb.at[d, pl.ds(3 * x, 3)], sb.at[i], rb.at[i], zb_ss.at[i], zb_rs.at[i])
        for i in range(2)
    ]

    def step_a(step):
        for ring in rings_a:
            ring.step(step)

    def step_b(step):
        for ring in rings_b:
            ring.step(step, split=step == 3)

    order = (4, 3, -3, 2, -2, 1, -1, 0)
    send(0)
    forward(0, 1, 2)
    send(1)
    forward(0, 2)
    gathered(0)
    loads[2].wait()
    loads[3].wait()
    part_a((0, 1), xa_s, xo, enc)
    for k in order[:2]:
        xa_copy(k, 0).start()
    forward(1, 1, 5)
    part_b((0, 1))
    for ring in rings_b:
        ring.first(0, 2, 0)
    forward(1, 5)
    gathered(1)
    loads[4].wait()
    loads[5].wait()
    part_b((2,))
    for ring in rings_b:
        ring.first(2, 3, 4)
    part_a((2,), xa_s, xo, enc)
    for k in order[:2]:
        xa_copy(k, 1).start()
    for k in order[2:]:
        for g in range(2):
            xa_copy(k, g).start()
    for ring in rings_b:
        ring.second(0, 2, 0)
    part_a((0, 1, 2), pa, xh, lambda v: v)

    def take_x(k):
        d = zp(k)
        remote(xa_s.at[d], xa_r.at[d], xa_ss, xa_rs.at[d], x_dev).wait_recv()
        hop(pa.at[d], pa.at[d], (xa_r.at[d],), 0, 2)

    for ring in rings_b:
        ring.second(2, 3, 4)
    take_x(4)
    step_a(1)
    for s, ks in ((2, (3, -3)), (3, (2, -2))):
        step_b(s + 1)
        for k in ks:
            take_x(k)
        step_a(s)
    rings_b[0].finish(xb_s)
    xb_copy = remote(xb_s, xb_r, xb_ss, xb_rs, x_dev)
    xb_copy.start()
    for k in (1, -1):
        take_x(k)
    step_a(4)
    take_x(0)
    own_b = pb.at[z, pl.ds(3 * xh, 3)]
    rings_b[1].finish(own_b)

    def local(src, dst, n, base):
        for i in range(n):
            gate, up, cap_grad = src[0, :, tile(i)], src[1, :, tile(i)], src[2, :, tile(i)]
            at = 2 * (base + i)
            codes = jnp.concatenate([cap_in[at : at + 1, :], cap_in[at + 1 : at + 2, :]], axis=1)
            cap = codes.astype(F32) * (1.0 / 512.0)
            sig = 1.0 / (1.0 + jnp.exp(-gate))
            act = gate * sig
            squash = jnp.tanh(act * up / cap)
            hid_grad = cap_grad * (1.0 - squash * squash)
            dst[0, :, tile(i)] = (cap * squash).astype(BF16)
            dst[1, :, tile(i)] = (hid_grad * up * sig * (1.0 + gate * (1.0 - sig))).astype(BF16)
            dst[2, :, tile(i)] = (hid_grad * act).astype(BF16)

    def halves(blk, step, d, width):
        return blk.at[:, :, pl.ds(d * (width // 2), width // 2)] if step == 4 else blk

    def gza_copy(i, step, d, got=False):
        blk = ga.at[zp((step if got else step - 1) * (1, -1)[d]), xh, :, :, cols_a[i]]
        blk = halves(blk, step, d, ha)
        return remote(blk, blk, gza_ss.at[step // 4], gza_rs.at[i, d, step - 1], z_dev[d])

    def phase(k):
        return 0 if abs(k) < 3 else 1 if abs(k) == 3 else 2

    def gxa_copy(i, k):
        blk = ga.at[zp(k), xh, :, :, cols_a[i]]
        return remote(blk, blk, gxa_ss, gxa_rs.at[phase(k)], x_dev)

    def gzb_copy(i, step, d, got=False):
        blk = gb.at[zp((step if got else step - 1) * (1, -1)[d]), pl.ds(3 * xs[i], 3)]
        blk = halves(blk, step, d, wb)
        return remote(blk, blk, gzb_ss.at[step // 4], gzb_rs.at[i, d, step - 1], z_dev[d])

    xb_copy.wait()
    hop(own_b, own_b, (xb_r,), 0, 2)
    local(own_b, gb.at[z, pl.ds(3 * xh, 3)], nb, na)

    def gxb_copy(x):
        blk = gb.at[z, pl.ds(3 * x, 3)]
        return remote(blk, blk, gxb_ss, gxb_rs, x_dev)

    gxb_copy(xh).start()
    for d in range(2):
        gzb_copy(1, 1, d).start()
    for i in range(2):
        own_a = pa.at[z, :, :, cols_a[i]]
        rings_a[i].finish(own_a)
        local(own_a, ga.at[z, xh, :, :, cols_a[i]], na // 2, i * (na // 2))
        for d in range(2):
            gza_copy(i, 1, d).start()
        gxa_copy(i, 0).start()

    def keep_a(k, x):
        d = zp(k)
        t = pl.multiple_of((d * 2 + x) * NB, NB)
        return pltpu.make_async_copy(ga.at[d, x], d_out.at[:, pl.ds(t, NB), pl.ds(0, wa)], dsem.at[0])

    def keep_b(k, x):
        d = zp(k)
        t = pl.multiple_of((d * 2 + x) * NB, NB)
        return pltpu.make_async_copy(
            gb.at[d, pl.ds(3 * x, 3)], d_out.at[:, pl.ds(t, NB), pl.ds(wa, wb)], dsem.at[1]
        )

    def keep_bs(k):
        for x in range(2):
            keep_b(k, x).start()

    keep_a(0, xh).start()
    keep_panel = pltpu.make_async_copy(panel, panel_out, lsem.at[0])
    keep_panel.start()

    def ig_rows(ks, a=True, b=True):
        def rows(ref):
            return jnp.concatenate([ref(zp(k), x) for k in ks for x in range(2)], axis=0)

        v = 0.0
        for m, wt in ((1, gw), (2, uw)):
            if a:
                v = v + dot(rows(lambda d, x: ga[d, x, m]), wt[:, :wa], 1, 1)
            if b:
                v = v + dot(rows(lambda d, x: gb[d, 3 * x + m]), wt[:, wa:], 1, 1)
        for n_k, k in enumerate(ks):
            part = v[n_k * 2 * NB : (n_k + 1) * 2 * NB].reshape(2, NB, 512)
            ig_acc[zp(k)] = part if b else ig_acc[zp(k)] + part
        if not a:
            return
        for k in ks:
            d = zp(k)
            sib_s[d] = ig_acc[d, 1 - core].astype(BF16)
            sib_copy(k).start()

    def ig_send(ks, n):
        blocks = sib_s.at[pl.ds(0, len(ks))]
        remote(blocks, blocks, sib_ss, sib_rs.at[n], sib_dev).wait_recv()
        for k in ks:
            d = zp(k)
            ig_s[d] = (ig_acc[d, core] + sib_r[d].astype(F32)).astype(BF16)

            @pl.when(d != q)
            def _():
                ig_copy((d - q + 8) % 8).start()

    def ig_copy(j):
        return remote(ig_s.at[chip(j)], ig_out.at[j], ig_ss, ig_rs, peer(j))

    def sib_copy(k):
        d = zp(k)
        return remote(sib_s.at[d], sib_r.at[d], sib_ss, sib_rs.at[phase(k)], sib_dev)

    def take_gx(ks, n):
        blocks = xa_s.at[pl.ds(0, len(ks))]
        remote(blocks, blocks, gxa_ss, gxa_rs.at[n], x_dev).wait_recv()
        for k in ks:
            keep_a(k, xo).start()

    def forward_a(step):
        for i in range(2):
            for d in range(2):
                k = (step - 1) * (1, -1)[d]
                gza_copy(i, step - 1, d, True).wait_recv()
                gza_copy(i, step, d).start()
                gxa_copy(i, k).start()
                if i == 1:
                    keep_a(k, xh).start()

    def forward_b(i, step):
        for d in range(2):
            gzb_copy(i, step - 1, d, True).wait_recv()
            gzb_copy(i, step, d).start()
            keep_b((step - 1) * (1, -1)[d], xs[i]).start()

    forward_a(2)
    gxb_copy(xo).wait_recv()
    for d in range(2):
        gzb_copy(0, 1, d).start()
    keep_bs(0)
    forward_b(1, 2)
    forward_a(3)
    forward_b(0, 2)
    forward_b(1, 3)
    forward_a(4)
    forward_b(0, 3)
    forward_b(1, 4)

    def sent(ref, sem):
        remote(ref, ref, sem, gxb_rs, x_dev).wait_send()

    sent(panel.at[0, pl.ds(0, 7)], tok_ss)
    sent(panel.at[0], fwd_ss)
    sent(xa_s, xa_ss)
    for ring in rings_a + rings_b:
        ring.drain()
    early = (0, 1, -1, 2, -2)
    take_gx(early, 0)
    ig_rows(early)
    for i in range(2):
        for d in range(2):
            gza_copy(i, 4, d, True).wait_recv()
        gxa_copy(i, 4).start()
    keep_a(4, xh).start()
    forward_b(0, 4)
    ig_send(early, 0)
    take_gx((3, -3), 1)
    ig_rows((3, -3))
    ig_send((3, -3), 1)
    for i in (1, 0):
        for d in range(2):
            gzb_copy(i, 4, d, True).wait_recv()
    keep_bs(4)
    ig_rows((4,), a=False)
    take_gx((4,), 2)
    ig_rows((4,), b=False)
    ig_send((4,), 2)
    last = pltpu.make_async_copy(ig_s.at[q], ig_out.at[0], lsem.at[1])
    last.start()

    sent(xa_s, gxa_ss)
    sent(sib_s, sib_ss)
    sent(sa.at[:, 0, 0], gza_ss.at[1])
    sent(sa.at[:, :, pl.ds(0, 3)], gza_ss.at[0])
    sent(sb.at[:, 0, 0], gzb_ss.at[1])
    sent(sb.at[:, :, pl.ds(0, 3)], gzb_ss.at[0])
    gxb_copy(xh).wait_send()

    pieces = pl.ds(0, 7)
    remote(ig_s.at[pieces], ig_out.at[pl.ds(1, 7)], ig_ss, ig_rs, x_dev).wait()
    pltpu.make_async_copy(ga, ga, dsem.at[0]).wait()
    pltpu.make_async_copy(gb, gb, dsem.at[1]).wait()
    keep_panel.wait()
    last.wait()


def weight_grads(
    d_in, panel_in, ig_in, ig_out, gg_out, ug_out, dg_out, d, panel, gg, ug, dg, ig_v, ig_b, isem, osem
):
    first, rest = pl.ds(0, 2 * TILE), pl.ds(2 * TILE, d.shape[2] - 2 * TILE)
    loads = []
    for src, dst in (
        (panel_in.at[0], panel.at[0]),
        (d_in.at[1, :, first], d.at[1, :, first]),
        (d_in.at[1, :, rest], d.at[1, :, rest]),
        (d_in.at[2], d.at[2]),
        (panel_in.at[1], panel.at[1]),
        (d_in.at[0], d.at[0]),
        (ig_in, ig_v),
    ):
        loads.append(pltpu.make_async_copy(src, dst, isem.at[len(loads)]))
        loads[-1].start()
    n = d.shape[2] // TILE
    stores = []

    def store(src, dst):
        stores.append(pltpu.make_async_copy(src, dst, osem.at[len(stores)]))
        stores[-1].start()

    loads[0].wait()
    loads[1].wait()
    for m, dst, out in ((1, gg, gg_out), (2, ug, ug_out)):
        for i in range(n):
            if (m, i) == (1, 2):
                loads[2].wait()
            if (m, i) == (2, 0):
                loads[3].wait()
            c = pl.ds(i * TILE, TILE)
            dst[:, c] = dot(panel[0], d[m, :, c], 0, 0).astype(BF16)
        store(dst, out)
    loads[6].wait()
    ig_b[...] = sum(ig_v[j].astype(F32) for j in range(8)).astype(BF16)
    store(ig_b, ig_out)
    loads[4].wait()
    loads[5].wait()
    for lo, hi in ((0, 4), (4, 6), (6, 7)):
        for i in range(lo, hi):
            c = pl.ds(i * TILE, TILE)
            dg[c, :] = dot(d[0, :, c], panel[1], 0, 0).astype(BF16)
        rows = pl.ds(lo * TILE, (hi - lo) * TILE)
        store(dg.at[rows], dg_out.at[rows])
    for c in stores:
        c.wait()


def per_device(tokens, out_grad, gate_weight, up_weight, down_weight, cap_codes):
    hidden = gate_weight.shape[1]
    n = hidden // TILE
    na = 4
    nb = n - na
    wa, wb = na * TILE, nb * TILE
    dma = pltpu.SemaphoreType.DMA
    sh = jax.ShapeDtypeStruct
    scratch = [
        pltpu.VMEM((512, hidden), BF16),
        pltpu.VMEM((512, hidden), BF16),
        pltpu.VMEM((hidden, 512), BF16),
        pltpu.VMEM((2, NZ, 2, NB, 512), BF16),
        pltpu.VMEM((hidden // 128, 128), jnp.int32),
        pltpu.VMEM((NZ, 3, NB, wa), F32),
        pltpu.VMEM((NZ, 6, NB, wb), F32),
        pltpu.VMEM((NZ, 3, NB, wa), BF16),
        pltpu.VMEM((NZ, 3, NB, wa), BF16),
        pltpu.VMEM((2, 2, 4, 3, NB, wa // 2), BF16),
        pltpu.VMEM((2, 2, 4, 3, NB, wa // 2), BF16),
        pltpu.VMEM((2, 2, 4, 3, NB, wb), BF16),
        pltpu.VMEM((2, 2, 4, 3, NB, wb), BF16),
        pltpu.VMEM((3, NB, wb), BF16),
        pltpu.VMEM((3, NB, wb), BF16),
        pltpu.VMEM((NZ, 2, 3, NB, wa), BF16),
        pltpu.VMEM((NZ, 6, NB, wb), BF16),
        pltpu.VMEM((NZ, 2, NB, 512), F32),
        pltpu.VMEM((NZ, NB, 512), BF16),
        pltpu.VMEM((NZ, NB, 512), BF16),
        pltpu.VMEM((NZ, NB, 512), BF16),
        dma((6,)), dma((2,)),
        dma, dma((2, 8)),
        dma, dma((2,)),
        dma, dma((NZ,)),
        dma((2, 2)), dma((2, 2, 4)),
        dma((2, 2)), dma((2, 2, 6)),
        dma, dma,
        dma, dma((3,)),
        dma((2,)), dma((2, 2, 4)),
        dma((2,)), dma((2, 2, 4)),
        dma, dma,
        dma, dma((3,)),
        dma, dma,
    ]
    any_spec = pl.BlockSpec(memory_space=pl.ANY)
    deltas, panel, ig_sum = pl.pallas_call(
        functools.partial(kernel, na, nb),
        out_shape=(sh((3, 512, hidden), BF16), sh((2, NZ, 2, NB, 512), BF16), sh((8, NB, 512), BF16)),
        in_specs=[any_spec] * 6,
        out_specs=[any_spec] * 3,
        scratch_shapes=scratch,
        compiler_params=pltpu.CompilerParams(
            collective_id=0, has_side_effects=True, vmem_limit_bytes=60 << 20
        ),
        name="exchange",
    )(tokens, out_grad, gate_weight, up_weight, down_weight, cap_codes.reshape(hidden // 128, 128))
    return pl.pallas_call(
        weight_grads,
        out_shape=(
            sh((NB, 512), BF16),
            sh((512, hidden), BF16),
            sh((512, hidden), BF16),
            sh((hidden, 512), BF16),
        ),
        in_specs=[any_spec] * 3,
        out_specs=(any_spec,) * 4,
        scratch_shapes=[
            pltpu.VMEM((3, 512, hidden), BF16),
            pltpu.VMEM((2, 512, 512), BF16),
            pltpu.VMEM((512, hidden), BF16),
            pltpu.VMEM((512, hidden), BF16),
            pltpu.VMEM((hidden, 512), BF16),
            pltpu.VMEM((8, NB, 512), BF16),
            pltpu.VMEM((NB, 512), BF16),
            dma((7,)),
            dma((6,)),
        ],
        compiler_params=pltpu.CompilerParams(vmem_limit_bytes=60 << 20),
        name="weight_grads",
    )(deltas, panel.reshape(2, 512, 512), ig_sum)


def solution(mesh):
    return jax.shard_map(
        per_device,
        mesh=mesh,
        in_specs=(
            P("hid", "wid"),
            P("hid", "wid"),
            P("wid", "hid"),
            P("wid", "hid"),
            P("hid", "wid"),
            P("hid"),
        ),
        out_specs=(P("hid", "wid"), P("wid", "hid"), P("wid", "hid"), P("hid", "wid")),
        check_vma=False,
    )
```
